256 devices in a mesh: seq: 32 (over x, y, core), head: 8 (over z).
Axes of the slice: x: 4, y: 4, z: 8, core: 2. Of those that a mesh axis runs over, the one named last changes fastest.
Arguments:
- layer_input: bfloat16 [32768, 6144], P('seq', 'head'), may hold values from -6 to 6
- queries: bfloat16 [32768, 4096], P('seq', 'head'), may hold values from -6 to 6
- keys: bfloat16 [32768, 4096], P('seq', 'head'), may hold values from -6 to 6
- values: bfloat16 [32768, 4096], P('seq', 'head'), may hold values from -6 to 6
- out_grad: bfloat16 [32768, 4096], P('seq', 'head'), may hold values from -6 to 6
Outputs:
- query_grad: bfloat16 [32768, 4096], P('seq', 'head')
- key_grad: bfloat16 [32768, 4096], P('seq', 'head')
- weight_grad: float32 [6144, 4096], P('seq', 'head')
The draws below stay inside these ranges and needn't reach their ends.
All inputs are finite; a program needn't handle non-finite values.
Results may differ from the reference program's by a relative error of at most 0.024.
Values may be sent and summed in bfloat16 or wider, within the bound.
No kernel may reach another device: no remote copies, remote signals or barrier semaphores. Data moves between devices by JAX's collectives and lax.ppermute only.
A program may use at most 128 MiB of HBM per device.

```python
import math
import jax
import jax.numpy as jnp
from jax import lax

D = 6144
DH = 128
TOK_DEV = 1024
BLOCK = 512
HEADS = 32
TOKENS = 32768
N_SEQ = 32


def with_spikes(drawn, stream_key, source, target, blocks, factor):
    def block_of(axis_at):
        return (jnp.arange(drawn.shape[axis_at]) // (drawn.shape[axis_at] // blocks)).reshape((-1,) + (1,) * (drawn.ndim - 1 - axis_at))

    near = jax.random.permutation(stream_key, blocks)[block_of(target)]
    other_side = (block_of(target) + blocks // 2) % blocks
    return jnp.where((block_of(source) == near) | (block_of(source) == other_side), factor * drawn, drawn)


def block_scale(own_key, dims, cuts, smallest, top_value):
    def one(axis_at, shards_of):
        draws = jax.random.uniform(jax.random.fold_in(jax.random.fold_in(own_key, 6), axis_at), (shards_of,), jnp.float32, smallest / len(cuts), top_value / len(cuts))
        return jnp.repeat(jnp.exp(draws), dims[axis_at] // shards_of).reshape((-1,) + (1,) * (len(dims) - axis_at - 1))

    factor_of = one(*cuts[0])
    for cut in cuts[1:]:
        factor_of = factor_of * one(*cut)
    return factor_of


def bell_draw(own_key, shape, spread, bound, pieces=(), dtype=jnp.bfloat16):
    gain = block_scale(own_key, shape, pieces, -0.22, 0.18) if pieces else 1.0
    drawn = jax.random.normal(own_key, shape, jnp.float32) * spread * gain
    return jnp.minimum(jnp.maximum(drawn, -bound), bound).astype(dtype)


def noise_with(stream_key, extent, scale, most, cuts, heavy, kind=jnp.bfloat16):
    result = scale * jax.random.normal(stream_key, extent, jnp.float32)
    if cuts:
        result = result * block_scale(stream_key, extent, cuts, -0.22, 0.18)
    return jnp.clip(with_spikes(result, jax.random.fold_in(stream_key, 3), *heavy), -most, most).astype(kind)


def setup_inputs(seed: int = 0) -> dict:
    arg_keys = jax.random.split(jax.random.key(seed), 6)
    layer_input = noise_with(arg_keys[0], (TOKENS, D), 1.0, 6.0, ((0, 32), (1, 8)), (0, 1, 32, 2.75))
    queries = bell_draw(arg_keys[1], (TOKENS, HEADS * DH), 1.0, 6.0, ((0, 32), (1, 8)))
    keys = bell_draw(arg_keys[2], (TOKENS, HEADS * DH), 1.0, 6.0, ((0, 32), (1, 8)))
    values = bell_draw(arg_keys[3], (TOKENS, HEADS * DH), 1.0, 6.0, ((0, 32), (1, 8)))
    out_grad = bell_draw(arg_keys[4], (TOKENS, HEADS * DH), 1.0, 6.0, ((0, 32), (1, 8)))
    return {"layer_input": layer_input, "queries": queries, "keys": keys, "values": values, "out_grad": out_grad}


def round_trip(matrix):
    return lax.optimization_barrier(matrix.astype(jnp.bfloat16)).astype(jnp.float32)

def head_grads(query_head, key_head, value_head, grad_head, scaling):
    shape = (TOKENS // BLOCK, BLOCK, DH)
    query_b = query_head.astype(jnp.float32).reshape(shape)
    key_b = key_head.astype(jnp.float32).reshape(shape)
    value_b = value_head.astype(jnp.float32).reshape(shape)
    grad_b = grad_head.astype(jnp.float32).reshape(shape)
    kv_blocks = jnp.einsum('nsd,nse->nde', key_b, value_b)
    grad_blocks = jnp.einsum('nsd,nse->nde', query_b, grad_b)
    before = jnp.cumsum(kv_blocks, 0) - kv_blocks
    after = lax.optimization_barrier(jnp.sum(grad_blocks, 0)) - jnp.cumsum(grad_blocks, 0)
    before16 = round_trip(before)
    after16 = round_trip(after)
    rows_idx = lax.broadcasted_iota(jnp.int32, (BLOCK, BLOCK), 0)
    cols_idx = lax.broadcasted_iota(jnp.int32, (BLOCK, BLOCK), 1)
    lower_mask = cols_idx <= rows_idx
    upper_mask = cols_idx >= rows_idx
    lower = round_trip(jnp.where(lower_mask, jnp.einsum('nsd,ntd->nst', grad_b, value_b), 0.0))
    upper = round_trip(jnp.where(upper_mask, jnp.einsum('nsd,ntd->nst', value_b, grad_b), 0.0))
    cross = round_trip(jnp.where(upper_mask, jnp.einsum('nsd,ntd->nst', key_b, query_b), 0.0))
    query_grad = jnp.einsum('nst,ntd->nsd', lower, key_b) + jnp.einsum('nse,nde->nsd', grad_b, before16)
    key_grad = jnp.einsum('nst,ntd->nsd', upper, query_b) + jnp.einsum('nse,nde->nsd', value_b, after16)
    value_grad = jnp.einsum('nst,nte->nse', cross, grad_b) + jnp.einsum('nsd,nde->nse', key_b, after16)
    outputs = []
    for matrix in (query_grad, key_grad, value_grad):
        outputs.append((matrix * scaling).reshape(TOKENS, DH).astype(jnp.bfloat16))
    return tuple(outputs)

def reference(layer_input, queries, keys, values, out_grad):
    scaling = 1.0 / math.sqrt(DH * TOKENS)

    def by_head(matrix):
        return matrix.reshape(TOKENS, HEADS, DH).transpose(1, 0, 2)

    def run_head(members):
        return head_grads(members[0], members[1], members[2], members[3], scaling)
    query_grad, key_grad, value_grad = lax.map(run_head, (by_head(queries), by_head(keys), by_head(values), by_head(out_grad)))

    def back(matrix):
        return matrix.transpose(1, 0, 2).reshape(TOKENS, HEADS * DH)
    query_grad = back(query_grad)
    key_grad = back(key_grad)
    value_grad = back(value_grad)
    weight_scale = 1.0 / math.sqrt(TOKENS)
    input_ranges = layer_input.reshape(N_SEQ, TOK_DEV, D)
    grad_ranges = value_grad.reshape(N_SEQ, TOK_DEV, HEADS * DH)

    def accumulate(total, members):
        partial_term = jnp.dot(members[0].T, members[1], preferred_element_type=jnp.float32) * weight_scale
        return (total + round_trip(partial_term), None)
    weight_grad, _ = lax.scan(accumulate, jnp.zeros((D, HEADS * DH), jnp.float32), (input_ranges, grad_ranges))
    return (query_grad, key_grad, weight_grad)
```

```python
import functools
import math

import jax
import jax.numpy as jnp
from jax import lax
from jax.experimental import pallas as pl
from jax.experimental.pallas import tpu as pltpu
from jax.sharding import PartitionSpec as P

DH = 128
BLOCK = 512
HALF = BLOCK // 2
NX, NY, NC = 4, 4, 2
BF16 = jnp.bfloat16
F32 = jnp.float32

NN = (((1,), (0,)), ((), ()))
NT = (((1,), (1,)), ((), ()))
TN = (((0,), (0,)), ((), ()))


def dot(a, b, dims):
    return lax.dot_general(a, b, dims, preferred_element_type=F32)


def params(mib):
    return pltpu.CompilerParams(vmem_limit_bytes=mib * 1024 * 1024)


def states_kernel(q_ref, k_ref, v_ref, o_ref, kv_ref, g_ref, tot_ref):
    kv = []
    g = []
    for b in range(2):
        rows = pl.ds(b * BLOCK, BLOCK)
        kv.append(dot(k_ref[rows, :], v_ref[rows, :], TN))
        g.append(dot(q_ref[rows, :], o_ref[rows, :], TN))
    kv_ref[0] = kv[0]
    g_ref[0] = g[1]
    tot_ref[0, 0] = (g[0] + g[1]).astype(BF16)
    tot_ref[1, 0] = (kv[0] + kv[1]).astype(BF16)


def local_states(q, k, v, o):
    heads = q.shape[1] // DH
    by_head = pl.BlockSpec((q.shape[0], DH), lambda h: (0, h))
    state = pl.BlockSpec((1, DH, DH), lambda h: (h, 0, 0))
    return pl.pallas_call(
        states_kernel,
        grid=(heads,),
        in_specs=[by_head] * 4,
        out_specs=[state, state, pl.BlockSpec((2, 1, DH, DH), lambda h: (0, h, 0, 0))],
        out_shape=[
            jax.ShapeDtypeStruct((heads, DH, DH), F32),
            jax.ShapeDtypeStruct((heads, DH, DH), F32),
            jax.ShapeDtypeStruct((2, heads, DH, DH), BF16),
        ],
        compiler_params=params(32),
        cost_estimate=pl.CostEstimate(flops=3 * 10**8, bytes_accessed=5 * 10**6, transcendentals=0),
        name="states",
    )(q, k, v, o)


def keep(s0, t0, rows, cols, upper):
    s = lax.broadcasted_iota(jnp.int32, (rows, cols), 0) + s0
    t = lax.broadcasted_iota(jnp.int32, (rows, cols), 1) + t0
    return t >= s if upper else t <= s


def upper_product(a, b, c):
    top = dot(a[:HALF], b, NT)
    top = jnp.where(keep(0, 0, HALF, BLOCK, True), top, 0.0).astype(BF16)
    low = dot(a[HALF:], b[HALF:], NT)
    low = jnp.where(keep(0, 0, HALF, HALF, True), low, 0.0).astype(BF16)
    return jnp.concatenate([dot(top, c, NN), dot(low, c[HALF:], NN)], 0)


def lower_product(a, b, c):
    top = dot(a[:HALF], b[:HALF], NT)
    top = jnp.where(keep(0, 0, HALF, HALF, False), top, 0.0).astype(BF16)
    low = dot(a[HALF:], b, NT)
    low = jnp.where(keep(HALF, 0, HALF, BLOCK, False), low, 0.0).astype(BF16)
    return jnp.concatenate([dot(top, c[:HALF], NN), dot(low, c, NN)], 0)


def value_kernel(scaling, *refs):
    ins, outs = refs[:10], refs[10:]
    for half in range(2):
        q_ref, k_ref, o_ref, later_ref, g_ref = ins[5 * half : 5 * half + 5]
        later = later_ref[0].astype(F32)
        for b in range(2):
            rows = pl.ds(b * BLOCK, BLOCK)
            k = k_ref[rows, :]
            after = (later + g_ref[0]) if b == 0 else later
            total = upper_product(k, q_ref[rows, :], o_ref[rows, :])
            total = total + dot(k, after.astype(BF16), NN)
            outs[half][rows, :] = (total * scaling).astype(BF16)


def value_gradient(q, k, o, later, g, scaling):
    rows = q.shape[0]
    specs = []
    for half in range(2):
        by_head = pl.BlockSpec((rows, DH), lambda h, half=half: (0, 2 * half + h))
        state = pl.BlockSpec((1, DH, DH), lambda h, half=half: (2 * half + h, 0, 0))
        specs += [by_head, by_head, by_head, state, state]
    out = pl.BlockSpec((rows, DH), lambda h: (0, h))
    return pl.pallas_call(
        functools.partial(value_kernel, scaling),
        grid=(2,),
        in_specs=specs,
        out_specs=[out, out],
        out_shape=[jax.ShapeDtypeStruct((rows, 2 * DH), BF16)] * 2,
        compiler_params=params(40),
        cost_estimate=pl.CostEstimate(flops=2 * 10**9, bytes_accessed=5 * 10**6, transcendentals=0),
        name="value_gradient",
    )(q, k, o, later, g, q, k, o, later, g)


def query_key_kernel(scaling, q_ref, k_ref, v_ref, o_ref, later_ref, g_ref, before_ref, kv_ref, dq_ref, dk_ref):
    later = later_ref[0].astype(F32)
    earlier = before_ref[0].astype(F32)
    for b in range(2):
        rows = pl.ds(b * BLOCK, BLOCK)
        q, k, v, o = q_ref[rows, :], k_ref[rows, :], v_ref[rows, :], o_ref[rows, :]
        after = (later + g_ref[0]) if b == 0 else later
        before = earlier if b == 0 else (earlier + kv_ref[0])
        dq = lower_product(o, v, k) + dot(o, before.astype(BF16), NT)
        dk = upper_product(v, o, q) + dot(v, after.astype(BF16), NT)
        dq_ref[rows, :] = (dq * scaling).astype(BF16)
        dk_ref[rows, :] = (dk * scaling).astype(BF16)


def query_key_gradients(q, k, v, o, later, g, before, kv, scaling):
    rows = q.shape[0]
    heads = q.shape[1] // DH
    by_head = pl.BlockSpec((rows, DH), lambda h: (0, h))
    state = pl.BlockSpec((1, DH, DH), lambda h: (h, 0, 0))
    return pl.pallas_call(
        functools.partial(query_key_kernel, scaling),
        grid=(heads,),
        in_specs=[by_head] * 4 + [state] * 4,
        out_specs=[by_head, by_head],
        out_shape=[jax.ShapeDtypeStruct(q.shape, BF16)] * 2,
        compiler_params=params(40),
        cost_estimate=pl.CostEstimate(flops=4 * 10**9, bytes_accessed=7 * 10**6, transcendentals=0),
        name="query_key_gradients",
    )(q, k, v, o, later, g, before, kv)


def terms_kernel(scale, pairs, n_x, n_v, core_ref, *refs):
    xs, vs = refs[:n_x], refs[n_x : n_x + n_v]
    mine_ref, other_ref = refs[n_x + n_v :]
    first = core_ref[0] == 0
    for at, pair in enumerate(pairs):
        for h, (x, v) in enumerate(pair):
            term = dot(xs[x][...], vs[v][...], NN) * scale
            piece = term.shape[0] // 2
            top = term[:piece].astype(BF16)
            low = term[piece:].astype(BF16)
            mine_ref[0, h, at] = jnp.where(first, top, low)
            other_ref[0, h, at] = jnp.where(first, low, top)


def weight_terms(core, xs, vs, pairs, scale):
    rows, tokens = xs[0].shape
    cols = vs[0].shape[1]
    piece = rows // 4
    n = len(pairs)
    out = jax.ShapeDtypeStruct((2, 2, n, piece, cols), BF16)
    out_spec = pl.BlockSpec((1, 2, n, piece, cols), lambda r, c: (r, 0, 0, 0, 0))
    mine, other = pl.pallas_call(
        functools.partial(terms_kernel, scale, pairs, len(xs), len(vs)),
        grid_spec=pltpu.PrefetchScalarGridSpec(
            num_scalar_prefetch=1,
            grid=(2,),
            in_specs=[pl.BlockSpec((rows // 2, tokens), lambda r, c: (r, 0))] * len(xs)
            + [pl.BlockSpec((tokens, cols), lambda r, c: (0, 0))] * len(vs),
            out_specs=[out_spec, out_spec],
        ),
        out_shape=[out, out],
        compiler_params=params(40),
        cost_estimate=pl.CostEstimate(
            flops=n * 8 * 10**8, bytes_accessed=n * 3 * 10**6, transcendentals=0
        ),
        name="weight_terms",
    )(core, *xs, *vs)
    shape = (4, n, piece, cols)
    return mine.reshape(shape), other.reshape(shape)


def seq_index(x, y, c):
    return ((x % NX) * NY + (y % NY)) * NC + c


CHIPS = [(x, y, c) for x in range(NX) for y in range(NY) for c in range(NC)]
SWAP = [(seq_index(x, y, c), seq_index(x, y, 1 - c)) for x, y, c in CHIPS]


def y_shift(d):
    return [(seq_index(x, y, c), seq_index(x, y + d, c)) for x, y, c in CHIPS]


def x_to(targets, d):
    return [(seq_index(t - d, y, c), seq_index(t, y, c)) for t in targets for y in range(NY) for c in range(NC)]


def total(parts):
    acc = parts[0].astype(F32)
    for part in parts[1:]:
        acc = acc + part.astype(F32)
    return acc.astype(BF16)


def over_core_and_y(mine, other, y):
    received = lax.ppermute(other, "seq", SWAP)

    def of(at):
        at = lax.rem(at, NY)
        pick = functools.partial(lax.dynamic_index_in_dim, axis=0, keepdims=False)
        return total([pick(mine, at), pick(received, at)])

    parts = [lax.ppermute(of(y + d), "seq", y_shift(d)) for d in (2, 1, 3)]
    return total([of(y)] + parts)


def over_x(pieces, targets, x):
    parts = []
    for d in (2, 1, 3):
        send = pieces[0]
        for t, piece in zip(targets[1:], pieces[1:]):
            send = jnp.where(x == (t - d) % NX, piece, send)
        parts.append(lax.ppermute(send, "seq", x_to(targets, d)))
    own = pieces[0]
    for t, piece in zip(targets[1:], pieces[1:]):
        own = jnp.where(x == t, piece, own)
    return total([own] + parts)


SLOTS = {
    (0, 0): (0, 0, 0),
    (0, 1): (1, -1, 0),
    (1, 0): (-1, 1, 0),
    (1, 1): (4, None, None),
    (2, 0): (2, -1, 1),
    (2, 1): (-2, 1, -1),
    (3, 0): (3, -1, 2),
    (3, 1): (-3, 1, -2),
}


def owners(flip, nz):
    pairs = []
    for x, y, c in CHIPS:
        r2, h = divmod(y, 2)
        slot = h ^ flip
        for m in range(nz):
            d, di, dj = SLOTS[(x, slot)]
            if d == 4:
                di, dj = ((1, -3), (-1, 3))[h]
            i, j = (m + di) % nz, (m + dj) % nz
            pairs.append((seq_index(x, y, c) * nz + m, (4 * i + 2 * r2 + c) * nz + j))
    return pairs


def per_device(layer_input, queries, keys, values, out_grad):
    tok_rows, features = queries.shape
    heads = features // DH
    n_seq, n_z = lax.axis_size("seq"), lax.axis_size("head")
    scaling = 1.0 / math.sqrt(DH * tok_rows * n_seq)
    weight_scale = 1.0 / math.sqrt(tok_rows * n_seq)
    s = lax.axis_index("seq")
    z = lax.axis_index("head")
    x, y, c = s // (NY * NC), lax.rem(s // NC, NY), lax.rem(s, NC)
    up = [(i, (i + 1) % n_z) for i in range(n_z)]
    down = [(i, (i - 1) % n_z) for i in range(n_z)]

    x_prev = lax.ppermute(layer_input, "head", up)
    x_next = lax.ppermute(layer_input, "head", down)

    kv0, g1, sums = local_states(queries, keys, values, out_grad)
    spread = sums.reshape(2, n_seq, heads * DH // n_seq, DH)
    gathered = lax.all_to_all(spread, "seq", 1, 1)
    at = lax.broadcasted_iota(jnp.int32, (n_seq, n_seq), 0)
    of = lax.broadcasted_iota(jnp.int32, (n_seq, n_seq), 1)
    chosen = jnp.stack([of > at, of < at]).astype(BF16)
    sums = jnp.einsum("kts,ksab->ktab", chosen, gathered, preferred_element_type=F32).astype(BF16)
    sums = lax.all_to_all(sums, "seq", 1, 1).reshape(2, heads, DH, DH)
    later, before = sums[0], sums[1]

    va, vb = value_gradient(queries, keys, out_grad, later, g1, scaling)
    ups, downs = [(va, vb)], [(va, vb)]
    for step in range(2):
        a, b = ups[-1]
        ups.append((lax.ppermute(a, "head", up), lax.ppermute(b, "head", up)))
        a, b = downs[-1]
        b = lax.ppermute(b, "head", down)
        downs.append((lax.ppermute(a, "head", down), b))
    up3 = lax.ppermute(ups[2][0], "head", up)
    down3 = lax.ppermute(downs[2][1], "head", down)

    query_grad, key_grad = query_key_gradients(
        queries, keys, values, out_grad, later, g1, before, kv0, scaling
    )

    core = c.astype(jnp.int32).reshape(1)
    xt, xt_prev, xt_next = layer_input.T, x_prev.T, x_next.T

    terms = weight_terms(
        core, [xt, xt_prev, xt_next], [va, vb], [[(i, 0), (i, 1)] for i in range(3)], weight_scale
    )
    p0 = over_core_and_y(*terms, y)
    near = [xt_prev, xt_next]
    ring = [[(0, 0), (0, 1)], [(1, 2), (1, 3)]]
    p1 = over_core_and_y(*weight_terms(core, near, [*downs[1], *ups[1]], ring, weight_scale), y)
    p2 = over_core_and_y(*weight_terms(core, near, [*downs[2], *ups[2]], ring, weight_scale), y)
    p3 = over_core_and_y(*weight_terms(core, near, [up3, down3], [[(1, 0), (0, 1)]], weight_scale), y)

    r0 = over_x([p0[:2], jnp.concatenate([p0[2:], p0[2:]], 0)], [0, 1], x)
    r1 = over_x([p1], [2], x)
    r2 = over_x([p2], [3], x)
    r3 = over_x([p3], [1], x)
    slot0 = jnp.where(x <= 1, r0[0], jnp.where(x == 2, r1[0], r2[0]))
    slot1 = jnp.where(x == 0, r0[1], jnp.where(x == 1, r3[0], jnp.where(x == 2, r1[1], r2[1])))

    h = lax.rem(y, 2)
    first = jnp.where(h == 0, slot0, slot1)
    second = jnp.where(h == 0, slot1, slot0)
    first = lax.ppermute(first, ("seq", "head"), owners(0, n_z))
    second = lax.ppermute(second, ("seq", "head"), owners(1, n_z))
    d = lax.rem(z - s // 4 + n_z, n_z)
    slot_one = (d == 1) | ((d >= 4) & (d <= 6))
    left = jnp.where(slot_one, second, first)
    right = jnp.where(slot_one, first, second)
    weight_grad = jnp.concatenate([left, right], 1).astype(F32)
    return (query_grad, key_grad, weight_grad)


def solution(mesh):
    return jax.shard_map(
        per_device,
        mesh=mesh,
        in_specs=(P("seq", "head"),) * 5,
        out_specs=(P("seq", "head"),) * 3,
        check_vma=False,
    )
```

```python
import functools
import math

import jax
import jax.numpy as jnp
from jax import lax
from jax.experimental import pallas as pl
from jax.experimental.pallas import tpu as pltpu
from jax.sharding import PartitionSpec as P

DH = 128
BLOCK = 512
HALF = BLOCK // 2
NX, NY, NC = 4, 4, 2
BF16 = jnp.bfloat16
F32 = jnp.float32

NN = (((1,), (0,)), ((), ()))
NT = (((1,), (1,)), ((), ()))
TN = (((0,), (0,)), ((), ()))


def dot(a, b, dims):
    return lax.dot_general(a, b, dims, preferred_element_type=F32)


QUICK = pl.CostEstimate(flops=1, bytes_accessed=1, transcendentals=0)


def params():
    return pltpu.CompilerParams(vmem_limit_bytes=58 * 1024 * 1024)


def tie(*arrays):
    return lax.optimization_barrier(arrays)


def states_kernel(_, q_ref, k_ref, v_ref, o_ref, kv_ref, g_ref, tot_ref, pack_ref):
    kv = []
    g = []
    for b in range(2):
        rows = pl.ds(b * BLOCK, BLOCK)
        kv.append(dot(k_ref[rows, :], v_ref[rows, :], TN))
        g.append(dot(q_ref[rows, :], o_ref[rows, :], TN))
    kv_ref[0] = kv[0]
    g_ref[0] = g[1]
    cut = tot_ref.shape[3]
    for p in range(DH // cut):
        rows = slice(p * cut, (p + 1) * cut)
        tot_ref[0, p, 0] = (g[0] + g[1])[rows].astype(BF16)
        tot_ref[0, p, 1] = (kv[0] + kv[1])[rows].astype(BF16)

    @pl.when(pl.program_id(0) < 2)
    def _():
        for p, ref in enumerate((q_ref, k_ref, o_ref)):
            pack_ref[p] = ref[...]


def local_states(core, q, k, v, o, n_seq):
    rows, features = q.shape
    heads = features // DH
    parts = n_seq // heads

    def head(h, c):
        return lax.rem(2 * (1 - c[0]) + h, heads)

    by_head = pl.BlockSpec((rows, DH), lambda h, c: (0, head(h, c)))
    state = pl.BlockSpec((1, DH, DH), lambda h, c: (head(h, c), 0, 0))
    cuts = (parts, 2, DH // parts, DH)
    return pl.pallas_call(
        states_kernel,
        grid_spec=pltpu.PrefetchScalarGridSpec(
            num_scalar_prefetch=1,
            grid=(heads,),
            in_specs=[by_head] * 4,
            out_specs=[
                state,
                state,
                pl.BlockSpec((1, *cuts), lambda h, c: (head(h, c), 0, 0, 0, 0)),
                pl.BlockSpec((3, rows, DH), lambda h, c: (0, 0, jnp.minimum(h, 1))),
            ],
        ),
        out_shape=[
            jax.ShapeDtypeStruct((heads, DH, DH), F32),
            jax.ShapeDtypeStruct((heads, DH, DH), F32),
            jax.ShapeDtypeStruct((heads, *cuts), BF16),
            jax.ShapeDtypeStruct((3, rows, 2 * DH), BF16),
        ],
        compiler_params=params(),
        cost_estimate=QUICK,
        name="states",
    )(core, q, k, v, o)


def sums_kernel(in_ref, out_ref):
    n = in_ref.shape[0]
    for which, order in ((0, range(n - 1, -1, -1)), (1, range(n))):
        acc = jnp.zeros(in_ref.shape[2:], F32)
        for at in order:
            part = acc.astype(BF16)
            out_ref[at, which] = part
            if which == 0:
                out_ref[at ^ 1, 2] = part
            acc = acc + in_ref[at, which].astype(F32)


def running_sums(parts):
    return pl.pallas_call(
        sums_kernel,
        out_shape=jax.ShapeDtypeStruct((parts.shape[0], 3, *parts.shape[2:]), BF16),
        compiler_params=params(),
        cost_estimate=QUICK,
        name="running_sums",
    )(parts)


def keep(s0, t0, rows, cols, upper):
    s = lax.broadcasted_iota(jnp.int32, (rows, cols), 0) + s0
    t = lax.broadcasted_iota(jnp.int32, (rows, cols), 1) + t0
    return t >= s if upper else t <= s


def upper_product(a, b, c):
    top = dot(a[:HALF], b, NT)
    top = jnp.where(keep(0, 0, HALF, BLOCK, True), top, 0.0).astype(BF16)
    low = dot(a[HALF:], b[HALF:], NT)
    low = jnp.where(keep(0, 0, HALF, HALF, True), low, 0.0).astype(BF16)
    return jnp.concatenate([dot(top, c, NN), dot(low, c[HALF:], NN)], 0)


def lower_product(a, b, c):
    top = dot(a[:HALF], b[:HALF], NT)
    top = jnp.where(keep(0, 0, HALF, HALF, False), top, 0.0).astype(BF16)
    low = dot(a[HALF:], b, NT)
    low = jnp.where(keep(HALF, 0, HALF, BLOCK, False), low, 0.0).astype(BF16)
    return jnp.concatenate([dot(top, c[:HALF], NN), dot(low, c, NN)], 0)


def value_kernel(scaling, _, *refs):
    own, other = refs[:3], refs[3:6]
    own_later, other_later, out_ref = refs[6:]

    def load(members, b):
        rows = pl.ds(b * BLOCK, BLOCK)
        return [ref[rows, :] if len(ref.shape) == 2 else ref[0, rows, :] for ref in members]

    for at, (members, later) in enumerate(((own, own_later), (other, other_later))):
        after = later[0, :, 0].reshape(DH, DH).astype(F32)
        for b in (1, 0):
            q, k, o = load(members, b)
            grad = upper_product(k, q, o) + dot(k, after.astype(BF16), NN)
            out_ref[at, pl.ds(b * BLOCK, BLOCK), :] = (grad * scaling).astype(BF16)
            if b == 1:
                after = after + dot(q, o, TN)


def value_gradient(core, q, k, o, packed, sums, scaling):
    rows = q.shape[0]
    parts, cut = sums.shape[1], sums.shape[3]
    own = pl.BlockSpec((rows, DH), lambda h, c: (0, 2 * c[0] + h))
    other = [pl.BlockSpec((1, rows, DH), lambda h, c, p=p: (p, 0, h)) for p in range(3)]
    later = [
        pl.BlockSpec((1, parts, 1, cut, DH), lambda h, c, k=k: (2 * c[0] + h, 0, k, 0, 0)) for k in (0, 2)
    ]
    out = pl.BlockSpec((2, rows, DH), lambda h, c: (0, 0, h))
    return pl.pallas_call(
        functools.partial(value_kernel, scaling),
        grid_spec=pltpu.PrefetchScalarGridSpec(
            num_scalar_prefetch=1,
            grid=(2,),
            in_specs=[own] * 3 + other + later,
            out_specs=out,
        ),
        out_shape=jax.ShapeDtypeStruct((2, rows, 2 * DH), BF16),
        compiler_params=params(),
        cost_estimate=QUICK,
        name="value_gradient",
    )(core, q, k, o, packed, packed, packed, sums, sums)


def query_key_kernel(scaling, q_ref, k_ref, v_ref, o_ref, later_ref, before_ref, g_ref, kv_ref, dq_ref, dk_ref):
    later = later_ref[0, :, 0].reshape(DH, DH).astype(F32)
    earlier = before_ref[0, :, 0].reshape(DH, DH).astype(F32)
    for b in range(2):
        rows = pl.ds(b * BLOCK, BLOCK)
        q, k, v, o = q_ref[rows, :], k_ref[rows, :], v_ref[rows, :], o_ref[rows, :]
        after = (later + g_ref[0]) if b == 0 else later
        before = earlier if b == 0 else (earlier + kv_ref[0])
        dq = lower_product(o, v, k) + dot(o, before.astype(BF16), NT)
        dk = upper_product(v, o, q) + dot(v, after.astype(BF16), NT)
        dq_ref[rows, :] = (dq * scaling).astype(BF16)
        dk_ref[rows, :] = (dk * scaling).astype(BF16)


def query_key_gradients(q, k, v, o, sums, g, kv, scaling):
    rows = q.shape[0]
    heads = q.shape[1] // DH
    parts, cut = sums.shape[1], sums.shape[3]
    by_head = pl.BlockSpec((rows, DH), lambda h: (0, h))
    state = pl.BlockSpec((1, DH, DH), lambda h: (h, 0, 0))
    later = pl.BlockSpec((1, parts, 1, cut, DH), lambda h: (h, 0, 0, 0, 0))
    earlier = pl.BlockSpec((1, parts, 1, cut, DH), lambda h: (h, 0, 1, 0, 0))
    return pl.pallas_call(
        functools.partial(query_key_kernel, scaling),
        grid=(heads,),
        in_specs=[by_head] * 4 + [later, earlier, state, state],
        out_specs=[by_head, by_head],
        out_shape=[jax.ShapeDtypeStruct(q.shape, BF16)] * 2,
        compiler_params=params(),
        cost_estimate=QUICK,
        name="query_key_gradients",
    )(q, k, v, o, sums, sums, g, kv)


def x_spec(tokens, rows, at):
    return pl.BlockSpec((tokens, rows // 2), at)


def terms_kernel(scale, blocks, n_x, n_v, *refs):
    xs, vs, out_ref = refs[:n_x], refs[n_x : n_x + n_v], refs[n_x + n_v]
    piece = out_ref.shape[2]
    for n, (x, v) in enumerate(blocks):
        term = dot(xs[2 * x][...], vs[v][0], TN) + dot(xs[2 * x + 1][...], vs[v][1], TN)
        for low in range(2):
            out_ref[low, n] = (term[low * piece : (low + 1) * piece] * scale).astype(BF16)


def weight_terms(xs, vs, blocks, scale):
    tokens, rows = xs[0].shape
    cols = vs[0].shape[2]
    tail = (len(blocks), rows // 4, cols)
    return pl.pallas_call(
        functools.partial(terms_kernel, scale, blocks, len(xs), len(vs)),
        grid=(2,),
        in_specs=[x_spec(tokens, rows, lambda r: (0, r))] * len(xs)
        + [pl.BlockSpec((2, tokens, cols), lambda r: (0, 0, 0))] * len(vs),
        out_specs=pl.BlockSpec((2, *tail), lambda r: (r, 0, 0, 0)),
        out_shape=jax.ShapeDtypeStruct((4, *tail), BF16),
        compiler_params=params(),
        cost_estimate=QUICK,
        name="weight_terms",
    )(*xs, *vs)


def last_kernel(scale, at_ref, *refs):
    xs, v_ref, outs = refs[:4], refs[4], refs[5:]
    piece = outs[0].shape[0]
    for core, pair in enumerate((xs[2:], xs[:2])):

        @pl.when(at_ref[1] == core)
        def _(pair=pair):
            term = dot(pair[0][...], v_ref[0], TN) + dot(pair[1][...], v_ref[1], TN)
            for low in range(2):
                place = lax.rem(2 * pl.program_id(0) + low + 4 - at_ref[0], 4)
                rounded = (term[low * piece : (low + 1) * piece] * scale).astype(BF16)
                for d in range(4):

                    @pl.when(place == d)
                    def _(d=d, rounded=rounded):
                        outs[d][...] = rounded


def last_terms(at, xs, v, scale):
    tokens, rows = xs[0].shape
    cols = v.shape[2]
    shape = (rows // 4, cols)

    def used_by(core):
        return lambda r, s: (0, jnp.where(s[1] == core, r, 0))

    return pl.pallas_call(
        functools.partial(last_kernel, scale),
        grid_spec=pltpu.PrefetchScalarGridSpec(
            num_scalar_prefetch=1,
            grid=(2,),
            in_specs=[x_spec(tokens, rows, used_by(1))] * 2
            + [x_spec(tokens, rows, used_by(0))] * 2
            + [pl.BlockSpec((2, tokens, cols), lambda r, s: (0, 0, 0))],
            out_specs=[pl.BlockSpec(shape, lambda r, s: (0, 0))] * 4,
        ),
        out_shape=[jax.ShapeDtypeStruct(shape, BF16)] * 4,
        compiler_params=params(),
        cost_estimate=QUICK,
        name="last_terms",
    )(at, *xs, v)


def seq_index(x, y, c):
    return ((x % NX) * NY + (y % NY)) * NC + c


CHIPS = [(x, y, c) for x in range(NX) for y in range(NY) for c in range(NC)]
SWAP = [(seq_index(x, y, c), seq_index(x, y, 1 - c)) for x, y, c in CHIPS]


def shift(axis, d):
    dx, dy = (d, 0) if axis == "x" else (0, d)
    return [(seq_index(x, y, c), seq_index(x + dx, y + dy, c)) for x, y, c in CHIPS]


def shift_to(axis, targets, d):
    at = {seq_index(x, y, c): (x if axis == "x" else y) for x, y, c in CHIPS}
    return [(a, b) for a, b in shift(axis, d) if at[b] in targets]


def total(parts):
    acc = parts[0].astype(F32)
    for part in parts[1:]:
        acc = acc + part.astype(F32)
    return acc.astype(BF16)


def send_all(axis, sums):
    return [lax.ppermute(sums[d], "seq", shift(axis, d)) for d in (2, 1, 3)]


def choose(pieces, targets, at):
    chosen = []
    for d in range(4):
        piece = pieces[0]
        for t, other in zip(targets[1:], pieces[1:]):
            piece = jnp.where(at == (t - d) % 4, other, piece)
        chosen.append(piece)
    return chosen


def send_to(axis, chosen, targets):
    return [lax.ppermute(chosen[d], "seq", shift_to(axis, targets, d)) for d in (2, 1, 3)]


HELD_AT_X = {0: ((-1, 1),) * 2, 1: ((1, -1),) * 2, 2: ((-1, 2),) * 2, 3: ((1, -2),) * 2}
HELD_AT_Y = {0: ((0, 0),) * 2, 1: ((-1, 0),) * 2, 2: ((1, 0),) * 2, 3: ((1, -3), (-1, 3))}
LAST = 3


def owners(turn, nz):
    pairs = ([], [])
    for x, y, c in CHIPS:
        by_x = c == turn
        r = y if by_x else x
        di, dj = HELD_AT_X[x][c] if by_x else HELD_AT_Y[y][c]
        for m in range(nz):
            i, j = (m + di) % nz, (m + dj) % nz
            pairs[not by_x and y == LAST].append((seq_index(x, y, c) * nz + m, (4 * i + r) * nz + j))
    return pairs


def per_device(layer_input, queries, keys, values, out_grad):
    tok_rows, features = queries.shape
    half = features // 2
    n_seq, n_z = lax.axis_size("seq"), lax.axis_size("head")
    scaling = 1.0 / math.sqrt(DH * tok_rows * n_seq)
    weight_scale = 1.0 / math.sqrt(tok_rows * n_seq)
    s = lax.axis_index("seq").astype(jnp.int32)
    z = lax.axis_index("head").astype(jnp.int32)
    x, y, c = s // (NY * NC), lax.rem(s // NC, NY), lax.rem(s, NC)
    core, at_x = c.reshape(1), jnp.stack([x, c])
    up = [(i, (i + 1) % n_z) for i in range(n_z)]
    down = [(i, (i - 1) % n_z) for i in range(n_z)]
    both = ("seq", "head")
    apart = [
        (seq_index(a, b, e) * n_z + m, seq_index(a, b, e) * n_z + (m + 1 - 2 * e) % n_z)
        for a, b, e in CHIPS
        for m in range(n_z)
    ]

    def go(array, way):
        return lax.ppermute(array, "head", way)

    def swap(array):
        return lax.ppermute(array, "seq", SWAP)

    def terms(xs, vs, blocks):
        return weight_terms(xs, vs, blocks, weight_scale)

    groups = {
        "x": [[seq_index(a, b, e) for a in range(NX)] for b in range(NY) for e in range(NC)],
        "y": [[seq_index(a, b, e) for b in range(NY)] for a in range(NX) for e in range(NC)],
    }

    def exchange(axis, pieces):
        return lax.all_to_all(pieces, "seq", 0, 0, axis_index_groups=groups[axis])

    prev0, next0 = go(layer_input, up), go(layer_input, down)
    kv0, g1, totals, packed = local_states(core, queries, keys, values, out_grad, n_seq)
    spread = lax.all_to_all(totals.reshape(n_seq, *totals.shape[2:]), "seq", 0, 0)
    sums = lax.all_to_all(running_sums(spread), "seq", 0, 0)
    sums = sums.reshape(*totals.shape[:2], *sums.shape[1:])
    packed = swap(packed)
    v0 = value_gradient(core, queries, keys, out_grad, packed, sums, scaling)

    u1, d1 = go(v0, up), go(v0, down)
    prev0, next0, kv0, x_own, _ = tie(prev0, next0, kv0, layer_input, v0)
    prev1, next1, own1 = swap(prev0), swap(next0), swap(x_own)
    query_grad, key_grad = query_key_gradients(queries, keys, values, out_grad, sums, g1, kv0, scaling)
    prev1, next1, query_grad, key_grad = tie(prev1, next1, query_grad, key_grad)
    near = [prev0, prev1, next0, next1]
    t0 = terms([x_own, own1, *near], [v0], [(0, 0), (1, 0), (2, 0)])

    p0 = exchange("x", t0)

    u1, d1 = tie(u1, d1, t0)[:2]
    u2, d2 = go(u1, up), go(d1, down)
    t1 = terms(near, [d1, u1], [(0, 0), (1, 1)])
    p0 = total(list(p0))
    p1 = exchange("y", t1)
    c0 = choose([p0[0], p0[1], p0[2]], [0, 1, 2], y)
    y0 = send_to("y", c0, [0, 1, 2])

    u2, d2 = tie(u2, d2, t1, *c0)[:2]
    v3 = lax.ppermute(jnp.where(c == 0, u2, d2), both, apart)
    t2 = terms(near, [d2, u2], [(0, 0), (1, 1)])
    p1 = total(list(p1))
    p2 = exchange("y", t2)

    v3 = tie(v3, t2, p1)[0]
    q3 = last_terms(at_x, near, v3, weight_scale)
    x3 = send_all("x", q3)
    *y0, p2, _ = tie(*y0, p2, q3[0])
    held = jnp.concatenate([p1, total(list(p2))], 0)
    x2 = exchange("x", held)
    r0 = total([c0[0]] + y0)
    p3 = total([q3[0]] + x3)

    p3 = tie(p3, held)[0]
    y3 = send_to("y", [p3] * 4, [LAST])
    held_x = total(list(x2))
    first = jnp.where(c == 0, held_x, r0)
    second = jnp.where(c == 0, r0, held_x)
    early0, late0 = owners(0, n_z)
    early1, late1 = owners(1, n_z)
    early_first = lax.ppermute(first, both, early0)
    early_second = lax.ppermute(second, both, early1)
    r3 = total([p3] + y3)
    r3 = tie(r3, first, second)[0]
    late_first = lax.ppermute(r3, both, late0)
    late_second = lax.ppermute(r3, both, late1)

    away = lax.rem(z - s // 4 + n_z, n_z)
    first = jnp.where(away == 4, late_first, early_first)
    second = jnp.where(away == 4, late_second, early_second)
    by_x = (away == 2) | (away == 3) | (away == 5) | (away == 6)
    left = jnp.where(by_x, first, second)
    right = jnp.where(by_x, second, first)
    weight_grad = jnp.concatenate([left, right], 1).astype(F32)
    return (query_grad, key_grad, weight_grad)


def solution(mesh):
    return jax.shard_map(
        per_device,
        mesh=mesh,
        in_specs=(P("seq", "head"),) * 5,
        out_specs=(P("seq", "head"),) * 3,
        check_vma=False,
    )
```

```python
import functools
import math

import jax
import jax.numpy as jnp
from jax import lax
from jax.experimental import pallas as pl
from jax.experimental.pallas import tpu as pltpu
from jax.sharding import PartitionSpec as P

DH = 128
BLOCK = 512
HALF = BLOCK // 2
NX, NY, NC = 4, 4, 2
BF16 = jnp.bfloat16
F32 = jnp.float32

NN = (((1,), (0,)), ((), ()))
NT = (((1,), (1,)), ((), ()))
TN = (((0,), (0,)), ((), ()))


def dot(a, b, dims):
    return lax.dot_general(a, b, dims, preferred_element_type=F32)


QUICK = pl.CostEstimate(flops=1, bytes_accessed=1, transcendentals=0)


def params():
    return pltpu.CompilerParams(vmem_limit_bytes=58 * 1024 * 1024)


def tie(*arrays):
    return lax.optimization_barrier(arrays)


def states_kernel(_, q_ref, k_ref, v_ref, o_ref, kv_ref, g_ref, tot_ref, pack_ref):
    kv = []
    g = []
    for b in range(2):
        rows = pl.ds(b * BLOCK, BLOCK)
        kv.append(dot(k_ref[rows, :], v_ref[rows, :], TN))
        g.append(dot(q_ref[rows, :], o_ref[rows, :], TN))
    kv_ref[0] = kv[0]
    g_ref[0] = g[1]
    cut = tot_ref.shape[3]
    for p in range(DH // cut):
        rows = slice(p * cut, (p + 1) * cut)
        tot_ref[0, p, 0] = (g[0] + g[1])[rows].astype(BF16)
        tot_ref[0, p, 1] = (kv[0] + kv[1])[rows].astype(BF16)

    @pl.when(pl.program_id(0) < 2)
    def _():
        for p, ref in enumerate((q_ref, k_ref, o_ref)):
            pack_ref[p] = ref[...]


def local_states(core, q, k, v, o, n_seq):
    rows, features = q.shape
    heads = features // DH
    parts = n_seq // heads

    def head(h, c):
        return lax.rem(2 * (1 - c[0]) + h, heads)

    by_head = pl.BlockSpec((rows, DH), lambda h, c: (0, head(h, c)))
    state = pl.BlockSpec((1, DH, DH), lambda h, c: (head(h, c), 0, 0))
    cuts = (parts, 2, DH // parts, DH)
    return pl.pallas_call(
        states_kernel,
        grid_spec=pltpu.PrefetchScalarGridSpec(
            num_scalar_prefetch=1,
            grid=(heads,),
            in_specs=[by_head] * 4,
            out_specs=[
                state,
                state,
                pl.BlockSpec((1, *cuts), lambda h, c: (head(h, c), 0, 0, 0, 0)),
                pl.BlockSpec((3, rows, DH), lambda h, c: (0, 0, jnp.minimum(h, 1))),
            ],
        ),
        out_shape=[
            jax.ShapeDtypeStruct((heads, DH, DH), F32),
            jax.ShapeDtypeStruct((heads, DH, DH), F32),
            jax.ShapeDtypeStruct((heads, *cuts), BF16),
            jax.ShapeDtypeStruct((3, rows, 2 * DH), BF16),
        ],
        compiler_params=params(),
        cost_estimate=QUICK,
        name="states",
    )(core, q, k, v, o)


def sums_kernel(in_ref, out_ref):
    n = in_ref.shape[0]
    for which, order in ((0, range(n - 1, -1, -1)), (1, range(n))):
        acc = jnp.zeros(in_ref.shape[2:], F32)
        for at in order:
            part = acc.astype(BF16)
            out_ref[at, which] = part
            if which == 0:
                out_ref[at ^ 1, 2] = part
            acc = acc + in_ref[at, which].astype(F32)


def running_sums(parts):
    return pl.pallas_call(
        sums_kernel,
        out_shape=jax.ShapeDtypeStruct((parts.shape[0], 3, *parts.shape[2:]), BF16),
        compiler_params=params(),
        cost_estimate=QUICK,
        name="running_sums",
    )(parts)


def keep(s0, t0, rows, cols, upper):
    s = lax.broadcasted_iota(jnp.int32, (rows, cols), 0) + s0
    t = lax.broadcasted_iota(jnp.int32, (rows, cols), 1) + t0
    return t >= s if upper else t <= s


def upper_product(a, b, c):
    top = dot(a[:HALF], b, NT)
    top = jnp.where(keep(0, 0, HALF, BLOCK, True), top, 0.0).astype(BF16)
    low = dot(a[HALF:], b[HALF:], NT)
    low = jnp.where(keep(0, 0, HALF, HALF, True), low, 0.0).astype(BF16)
    return jnp.concatenate([dot(top, c, NN), dot(low, c[HALF:], NN)], 0)


def lower_product(a, b, c):
    top = dot(a[:HALF], b[:HALF], NT)
    top = jnp.where(keep(0, 0, HALF, HALF, False), top, 0.0).astype(BF16)
    low = dot(a[HALF:], b, NT)
    low = jnp.where(keep(HALF, 0, HALF, BLOCK, False), low, 0.0).astype(BF16)
    return jnp.concatenate([dot(top, c[:HALF], NN), dot(low, c, NN)], 0)


def value_kernel(scaling, _, *refs):
    own, other = refs[:3], refs[3:6]
    own_later, other_later, out_ref = refs[6:]

    def load(members, b):
        rows = pl.ds(b * BLOCK, BLOCK)
        return [ref[rows, :] if len(ref.shape) == 2 else ref[0, rows, :] for ref in members]

    for at, (members, later) in enumerate(((own, own_later), (other, other_later))):
        after = later[0, :, 0].reshape(DH, DH).astype(F32)
        for b in (1, 0):
            q, k, o = load(members, b)
            grad = upper_product(k, q, o) + dot(k, after.astype(BF16), NN)
            out_ref[at, pl.ds(b * BLOCK, BLOCK), :] = (grad * scaling).astype(BF16)
            if b == 1:
                after = after + dot(q, o, TN)


def value_gradient(core, q, k, o, packed, sums, scaling):
    rows = q.shape[0]
    parts, cut = sums.shape[1], sums.shape[3]
    own = pl.BlockSpec((rows, DH), lambda h, c: (0, 2 * c[0] + h))
    other = [pl.BlockSpec((1, rows, DH), lambda h, c, p=p: (p, 0, h)) for p in range(3)]
    later = [
        pl.BlockSpec((1, parts, 1, cut, DH), lambda h, c, k=k: (2 * c[0] + h, 0, k, 0, 0)) for k in (0, 2)
    ]
    out = pl.BlockSpec((2, rows, DH), lambda h, c: (0, 0, h))
    return pl.pallas_call(
        functools.partial(value_kernel, scaling),
        grid_spec=pltpu.PrefetchScalarGridSpec(
            num_scalar_prefetch=1,
            grid=(2,),
            in_specs=[own] * 3 + other + later,
            out_specs=out,
        ),
        out_shape=jax.ShapeDtypeStruct((2, rows, 2 * DH), BF16),
        compiler_params=params(),
        cost_estimate=QUICK,
        name="value_gradient",
    )(core, q, k, o, packed, packed, packed, sums, sums)


def query_key_kernel(scaling, q_ref, k_ref, v_ref, o_ref, later_ref, before_ref, g_ref, kv_ref, dq_ref, dk_ref):
    later = later_ref[0, :, 0].reshape(DH, DH).astype(F32)
    earlier = before_ref[0, :, 0].reshape(DH, DH).astype(F32)
    for b in range(2):
        rows = pl.ds(b * BLOCK, BLOCK)
        q, k, v, o = q_ref[rows, :], k_ref[rows, :], v_ref[rows, :], o_ref[rows, :]
        after = (later + g_ref[0]) if b == 0 else later
        before = earlier if b == 0 else (earlier + kv_ref[0])
        dq = lower_product(o, v, k) + dot(o, before.astype(BF16), NT)
        dk = upper_product(v, o, q) + dot(v, after.astype(BF16), NT)
        dq_ref[rows, :] = (dq * scaling).astype(BF16)
        dk_ref[rows, :] = (dk * scaling).astype(BF16)


def query_key_gradients(q, k, v, o, sums, g, kv, scaling):
    rows = q.shape[0]
    heads = q.shape[1] // DH
    parts, cut = sums.shape[1], sums.shape[3]
    by_head = pl.BlockSpec((rows, DH), lambda h: (0, h))
    state = pl.BlockSpec((1, DH, DH), lambda h: (h, 0, 0))
    later = pl.BlockSpec((1, parts, 1, cut, DH), lambda h: (h, 0, 0, 0, 0))
    earlier = pl.BlockSpec((1, parts, 1, cut, DH), lambda h: (h, 0, 1, 0, 0))
    return pl.pallas_call(
        functools.partial(query_key_kernel, scaling),
        grid=(heads,),
        in_specs=[by_head] * 4 + [later, earlier, state, state],
        out_specs=[by_head, by_head],
        out_shape=[jax.ShapeDtypeStruct(q.shape, BF16)] * 2,
        compiler_params=params(),
        cost_estimate=QUICK,
        name="query_key_gradients",
    )(q, k, v, o, sums, sums, g, kv)


def x_spec(tokens, rows, at):
    return pl.BlockSpec((tokens, rows // 2), at)


def terms_kernel(scale, blocks, n_x, n_v, *refs):
    xs, vs, out_ref = refs[:n_x], refs[n_x : n_x + n_v], refs[n_x + n_v]
    piece = out_ref.shape[2]
    for n, (x, v) in enumerate(blocks):
        term = dot(xs[2 * x][...], vs[v][0], TN) + dot(xs[2 * x + 1][...], vs[v][1], TN)
        for low in range(2):
            out_ref[low, n] = (term[low * piece : (low + 1) * piece] * scale).astype(BF16)


def weight_terms(xs, vs, blocks, scale):
    tokens, rows = xs[0].shape
    cols = vs[0].shape[2]
    tail = (len(blocks), rows // 4, cols)
    return pl.pallas_call(
        functools.partial(terms_kernel, scale, blocks, len(xs), len(vs)),
        grid=(2,),
        in_specs=[x_spec(tokens, rows, lambda r: (0, r))] * len(xs)
        + [pl.BlockSpec((2, tokens, cols), lambda r: (0, 0, 0))] * len(vs),
        out_specs=pl.BlockSpec((2, *tail), lambda r: (r, 0, 0, 0)),
        out_shape=jax.ShapeDtypeStruct((4, *tail), BF16),
        compiler_params=params(),
        cost_estimate=QUICK,
        name="weight_terms",
    )(*xs, *vs)


def last_kernel(scale, at_ref, *refs):
    xs, v_ref, outs = refs[:4], refs[4], refs[5:]
    piece = outs[0].shape[0]
    for core, pair in enumerate((xs[2:], xs[:2])):

        @pl.when(at_ref[1] == core)
        def _(pair=pair):
            term = dot(pair[0][...], v_ref[0], TN) + dot(pair[1][...], v_ref[1], TN)
            for low in range(2):
                place = lax.rem(2 * pl.program_id(0) + low + 4 - at_ref[0], 4)
                rounded = (term[low * piece : (low + 1) * piece] * scale).astype(BF16)
                for d in range(4):

                    @pl.when(place == d)
                    def _(d=d, rounded=rounded):
                        outs[d][...] = rounded


def last_terms(at, xs, v, scale):
    tokens, rows = xs[0].shape
    cols = v.shape[2]
    shape = (rows // 4, cols)

    def used_by(core):
        return lambda r, s: (0, jnp.where(s[1] == core, r, 0))

    return pl.pallas_call(
        functools.partial(last_kernel, scale),
        grid_spec=pltpu.PrefetchScalarGridSpec(
            num_scalar_prefetch=1,
            grid=(2,),
            in_specs=[x_spec(tokens, rows, used_by(1))] * 2
            + [x_spec(tokens, rows, used_by(0))] * 2
            + [pl.BlockSpec((2, tokens, cols), lambda r, s: (0, 0, 0))],
            out_specs=[pl.BlockSpec(shape, lambda r, s: (0, 0))] * 4,
        ),
        out_shape=[jax.ShapeDtypeStruct(shape, BF16)] * 4,
        compiler_params=params(),
        cost_estimate=QUICK,
        name="last_terms",
    )(at, *xs, v)


def seq_index(x, y, c):
    return ((x % NX) * NY + (y % NY)) * NC + c


CHIPS = [(x, y, c) for x in range(NX) for y in range(NY) for c in range(NC)]
SWAP = [(seq_index(x, y, c), seq_index(x, y, 1 - c)) for x, y, c in CHIPS]


def shift(axis, d):
    dx, dy = (d, 0) if axis == "x" else (0, d)
    return [(seq_index(x, y, c), seq_index(x + dx, y + dy, c)) for x, y, c in CHIPS]


def shift_to(axis, targets, d):
    at = {seq_index(x, y, c): (x if axis == "x" else y) for x, y, c in CHIPS}
    return [(a, b) for a, b in shift(axis, d) if at[b] in targets]


def total(parts):
    acc = parts[0].astype(F32)
    for part in parts[1:]:
        acc = acc + part.astype(F32)
    return acc.astype(BF16)


def send_all(axis, sums):
    return [lax.ppermute(sums[d], "seq", shift(axis, d)) for d in (2, 1, 3)]


def choose(pieces, targets, at):
    chosen = []
    for d in range(4):
        piece = pieces[0]
        for t, other in zip(targets[1:], pieces[1:]):
            piece = jnp.where(at == (t - d) % 4, other, piece)
        chosen.append(piece)
    return chosen


def send_to(axis, chosen, targets):
    return [lax.ppermute(chosen[d], "seq", shift_to(axis, targets, d)) for d in (2, 1, 3)]


HELD_AT_X = ((2, 1), (-2, -1), (3, 2), (-3, -2))
HELD_AT_Y = ((0, 0), (1, 0), (-1, 0), (4, None))
LAST = 3
LAST_STEP = (-3, 3)


def to_x(d, nz):
    return [
        (seq_index(x, y, c) * nz + m, seq_index(x + d, y, c) * nz + (m + HELD_AT_X[(x + d) % NX][1]) % nz)
        for x, y, c in CHIPS
        for m in range(nz)
    ]


def to_last(d, nz):
    return [
        (seq_index(x, y, c) * nz + m, seq_index(x, LAST, c) * nz + (m + LAST_STEP[c]) % nz)
        for x, y, c in CHIPS
        for m in range(nz)
        if (y + d) % NY == LAST
    ]


def owners(turn, nz):
    pairs = []
    for x, y, c in CHIPS:
        by_x = c == turn
        r = y if by_x else x
        d = HELD_AT_X[x][0] if by_x else HELD_AT_Y[y][0]
        for j in range(nz):
            pairs.append((seq_index(x, y, c) * nz + j, (4 * ((j - d) % nz) + r) * nz + j))
    return pairs


def per_device(layer_input, queries, keys, values, out_grad):
    tok_rows, features = queries.shape
    half = features // 2
    n_seq, n_z = lax.axis_size("seq"), lax.axis_size("head")
    scaling = 1.0 / math.sqrt(DH * tok_rows * n_seq)
    weight_scale = 1.0 / math.sqrt(tok_rows * n_seq)
    s = lax.axis_index("seq").astype(jnp.int32)
    z = lax.axis_index("head").astype(jnp.int32)
    x, y, c = s // (NY * NC), lax.rem(s // NC, NY), lax.rem(s, NC)
    core, at_x = c.reshape(1), jnp.stack([x, c])
    up = [(i, (i + 1) % n_z) for i in range(n_z)]
    down = [(i, (i - 1) % n_z) for i in range(n_z)]
    both = ("seq", "head")
    apart = [
        (seq_index(a, b, e) * n_z + m, seq_index(a, b, e) * n_z + (m + 1 - 2 * e) % n_z)
        for a, b, e in CHIPS
        for m in range(n_z)
    ]

    def go(array, way):
        return lax.ppermute(array, "head", way)

    def swap(array):
        return lax.ppermute(array, "seq", SWAP)

    def terms(xs, vs, blocks):
        return weight_terms(xs, vs, blocks, weight_scale)

    groups = {
        "x": [[seq_index(a, b, e) for a in range(NX)] for b in range(NY) for e in range(NC)],
        "y": [[seq_index(a, b, e) for b in range(NY)] for a in range(NX) for e in range(NC)],
    }

    def exchange(axis, pieces):
        return lax.all_to_all(pieces, "seq", 0, 0, axis_index_groups=groups[axis])

    prev0, next0 = go(layer_input, up), go(layer_input, down)
    kv0, g1, totals, packed = local_states(core, queries, keys, values, out_grad, n_seq)
    spread = lax.all_to_all(totals.reshape(n_seq, *totals.shape[2:]), "seq", 0, 0)
    sums = lax.all_to_all(running_sums(spread), "seq", 0, 0)
    sums = sums.reshape(*totals.shape[:2], *sums.shape[1:])
    packed = swap(packed)
    v0 = value_gradient(core, queries, keys, out_grad, packed, sums, scaling)

    u1, d1 = go(v0, up), go(v0, down)
    prev0, next0, kv0, x_own, _ = tie(prev0, next0, kv0, layer_input, v0)
    prev1, next1, own1 = swap(prev0), swap(next0), swap(x_own)
    query_grad, key_grad = query_key_gradients(queries, keys, values, out_grad, sums, g1, kv0, scaling)
    prev1, next1, query_grad, key_grad = tie(prev1, next1, query_grad, key_grad)
    near = [prev0, prev1, next0, next1]
    t0 = terms([x_own, own1, *near], [v0], [(0, 0), (1, 0), (2, 0)])

    p0 = exchange("x", t0)

    u1, d1 = tie(u1, d1, t0)[:2]
    u2, d2 = go(u1, up), go(d1, down)
    t1 = terms(near, [d1, u1], [(0, 0), (1, 1)])
    p0 = total(list(tie(p0, t1)[0]))
    p1 = exchange("y", t1)
    c0 = choose([p0[0], p0[1], p0[2]], [0, 1, 2], y)
    y0 = send_to("y", c0, [0, 1, 2])

    u2, d2, *y0 = tie(u2, d2, *y0, t1)[:5]
    v3 = lax.ppermute(jnp.where(c == 0, u2, d2), both, apart)
    t2 = terms(near, [d2, u2], [(0, 0), (1, 1)])
    p1 = total(list(p1))
    p2 = exchange("y", t2)

    v3, p1, r0 = tie(v3, p1, total([c0[0]] + y0), t2)[:3]
    q3 = last_terms(at_x, near, v3, weight_scale)
    x3 = send_all("x", q3)
    p2 = total(list(tie(p2, q3[0])[0]))
    held = choose([p1[0], p1[1], p2[0], p2[1]], [0, 1, 2, 3], x)
    x2 = [lax.ppermute(held[d], both, to_x(d, n_z)) for d in (0, 2, 1, 3)]
    p3 = total([q3[0]] + x3)

    p3 = tie(p3, *held)[0]
    y3 = [lax.ppermute(p3, both, to_last(d, n_z)) for d in (0, 2, 1, 3)]
    held_x = total(x2)
    first = jnp.where(c == 0, held_x, r0)
    second = jnp.where(c == 0, r0, held_x)
    r3 = total(y3)
    last = y == LAST
    first = jnp.where((c == 1) & last, r3, first)
    second = jnp.where((c == 0) & last, r3, second)
    first = lax.ppermute(first, both, owners(0, n_z))
    second = lax.ppermute(second, both, owners(1, n_z))

    away = lax.rem(z - s // 4 + n_z, n_z)
    by_x = (away == 2) | (away == 3) | (away == 5) | (away == 6)
    left = jnp.where(by_x, first, second)
    right = jnp.where(by_x, second, first)
    weight_grad = jnp.concatenate([left, right], 1).astype(F32)
    return (query_grad, key_grad, weight_grad)


def solution(mesh):
    return jax.shard_map(
        per_device,
        mesh=mesh,
        in_specs=(P("seq", "head"),) * 5,
        out_specs=(P("seq", "head"),) * 3,
        check_vma=False,
    )
```

```python
import functools
import math

import jax
import jax.numpy as jnp
from jax import lax
from jax.experimental import pallas as pl
from jax.experimental.pallas import tpu as pltpu
from jax.sharding import PartitionSpec as P

DH = 128
BLOCK = 512
HALF = BLOCK // 2
NX, NY, NC = 4, 4, 2
BF16 = jnp.bfloat16
F32 = jnp.float32

NN = (((1,), (0,)), ((), ()))
NT = (((1,), (1,)), ((), ()))
TN = (((0,), (0,)), ((), ()))


def dot(a, b, dims):
    return lax.dot_general(a, b, dims, preferred_element_type=F32)


QUICK = pl.CostEstimate(flops=1, bytes_accessed=1, transcendentals=0)


def params(mib=58):
    return pltpu.CompilerParams(vmem_limit_bytes=mib * 1024 * 1024)


def tie(*arrays):
    return lax.optimization_barrier(arrays)


def states_kernel(_, q_ref, k_ref, v_ref, o_ref, kv_ref, g_ref, tot_ref, pack_ref):
    kv = []
    g = []
    for b in range(2):
        rows = pl.ds(b * BLOCK, BLOCK)
        kv.append(dot(k_ref[rows, :], v_ref[rows, :], TN))
        g.append(dot(q_ref[rows, :], o_ref[rows, :], TN))
    kv_ref[0] = kv[0]
    g_ref[0] = g[1]
    cut = tot_ref.shape[3]
    for p in range(DH // cut):
        rows = slice(p * cut, (p + 1) * cut)
        tot_ref[0, p, 0] = (g[0] + g[1])[rows].astype(BF16)
        tot_ref[0, p, 1] = (kv[0] + kv[1])[rows].astype(BF16)

    @pl.when(pl.program_id(0) < 2)
    def _():
        for p, ref in enumerate((q_ref, k_ref, o_ref)):
            pack_ref[p] = ref[...]


def local_states(core, q, k, v, o, n_seq):
    rows, features = q.shape
    heads = features // DH
    parts = n_seq // heads

    def head(h, c):
        return lax.rem(2 * (1 - c[0]) + h, heads)

    by_head = pl.BlockSpec((rows, DH), lambda h, c: (0, head(h, c)))
    state = pl.BlockSpec((1, DH, DH), lambda h, c: (head(h, c), 0, 0))
    cuts = (parts, 2, DH // parts, DH)
    return pl.pallas_call(
        states_kernel,
        grid_spec=pltpu.PrefetchScalarGridSpec(
            num_scalar_prefetch=1,
            grid=(heads,),
            in_specs=[by_head] * 4,
            out_specs=[
                state,
                state,
                pl.BlockSpec((1, *cuts), lambda h, c: (head(h, c), 0, 0, 0, 0)),
                pl.BlockSpec((3, rows, DH), lambda h, c: (0, 0, jnp.minimum(h, 1))),
            ],
        ),
        out_shape=[
            jax.ShapeDtypeStruct((heads, DH, DH), F32),
            jax.ShapeDtypeStruct((heads, DH, DH), F32),
            jax.ShapeDtypeStruct((heads, *cuts), BF16),
            jax.ShapeDtypeStruct((3, rows, 2 * DH), BF16),
        ],
        compiler_params=params(),
        cost_estimate=QUICK,
        name="states",
    )(core, q, k, v, o)


def sums_kernel(in_ref, out_ref):
    n = in_ref.shape[0]
    for which, order in ((0, range(n - 1, -1, -1)), (1, range(n))):
        acc = jnp.zeros(in_ref.shape[2:], F32)
        for at in order:
            part = acc.astype(BF16)
            out_ref[at, which] = part
            if which == 0:
                out_ref[at ^ 1, 2] = part
            acc = acc + in_ref[at, which].astype(F32)


def running_sums(parts):
    return pl.pallas_call(
        sums_kernel,
        out_shape=jax.ShapeDtypeStruct((parts.shape[0], 3, *parts.shape[2:]), BF16),
        compiler_params=params(),
        cost_estimate=QUICK,
        name="running_sums",
    )(parts)


def keep(s0, t0, rows, cols, upper):
    s = lax.broadcasted_iota(jnp.int32, (rows, cols), 0) + s0
    t = lax.broadcasted_iota(jnp.int32, (rows, cols), 1) + t0
    return t >= s if upper else t <= s


def upper_product(a, b, c):
    top = dot(a[:HALF], b, NT)
    top = jnp.where(keep(0, 0, HALF, BLOCK, True), top, 0.0).astype(BF16)
    low = dot(a[HALF:], b[HALF:], NT)
    low = jnp.where(keep(0, 0, HALF, HALF, True), low, 0.0).astype(BF16)
    return jnp.concatenate([dot(top, c, NN), dot(low, c[HALF:], NN)], 0)


def lower_product(a, b, c):
    top = dot(a[:HALF], b[:HALF], NT)
    top = jnp.where(keep(0, 0, HALF, HALF, False), top, 0.0).astype(BF16)
    low = dot(a[HALF:], b, NT)
    low = jnp.where(keep(HALF, 0, HALF, BLOCK, False), low, 0.0).astype(BF16)
    return jnp.concatenate([dot(top, c[:HALF], NN), dot(low, c, NN)], 0)


def value_kernel(scaling, _, *refs):
    own, other = refs[:3], refs[3:6]
    own_later, other_later, out_ref = refs[6:]

    def load(members, b):
        rows = pl.ds(b * BLOCK, BLOCK)
        return [ref[rows, :] if len(ref.shape) == 2 else ref[0, rows, :] for ref in members]

    for at, (members, later) in enumerate(((own, own_later), (other, other_later))):
        after = later[0, :, 0].reshape(DH, DH).astype(F32)
        for b in (1, 0):
            q, k, o = load(members, b)
            grad = upper_product(k, q, o) + dot(k, after.astype(BF16), NN)
            out_ref[at, pl.ds(b * BLOCK, BLOCK), :] = (grad * scaling).astype(BF16)
            if b == 1:
                after = after + dot(q, o, TN)


def value_gradient(core, q, k, o, packed, sums, scaling):
    rows = q.shape[0]
    parts, cut = sums.shape[1], sums.shape[3]
    own = pl.BlockSpec((rows, DH), lambda h, c: (0, 2 * c[0] + h))
    other = [pl.BlockSpec((1, rows, DH), lambda h, c, p=p: (p, 0, h)) for p in range(3)]
    later = [
        pl.BlockSpec((1, parts, 1, cut, DH), lambda h, c, k=k: (2 * c[0] + h, 0, k, 0, 0)) for k in (0, 2)
    ]
    out = pl.BlockSpec((2, rows, DH), lambda h, c: (0, 0, h))
    return pl.pallas_call(
        functools.partial(value_kernel, scaling),
        grid_spec=pltpu.PrefetchScalarGridSpec(
            num_scalar_prefetch=1,
            grid=(2,),
            in_specs=[own] * 3 + other + later,
            out_specs=out,
        ),
        out_shape=jax.ShapeDtypeStruct((2, rows, 2 * DH), BF16),
        compiler_params=params(52),
        cost_estimate=QUICK,
        name="value_gradient",
    )(core, q, k, o, packed, packed, packed, sums, sums)


def query_key_kernel(scaling, q_ref, k_ref, v_ref, o_ref, later_ref, before_ref, g_ref, kv_ref, dq_ref, dk_ref):
    later = later_ref[0, :, 0].reshape(DH, DH).astype(F32)
    earlier = before_ref[0, :, 0].reshape(DH, DH).astype(F32)
    for b in range(2):
        rows = pl.ds(b * BLOCK, BLOCK)
        q, k, v, o = q_ref[rows, :], k_ref[rows, :], v_ref[rows, :], o_ref[rows, :]
        after = (later + g_ref[0]) if b == 0 else later
        before = earlier if b == 0 else (earlier + kv_ref[0])
        dq = lower_product(o, v, k) + dot(o, before.astype(BF16), NT)
        dk = upper_product(v, o, q) + dot(v, after.astype(BF16), NT)
        dq_ref[rows, :] = (dq * scaling).astype(BF16)
        dk_ref[rows, :] = (dk * scaling).astype(BF16)


def query_key_gradients(q, k, v, o, sums, g, kv, scaling):
    rows = q.shape[0]
    heads = q.shape[1] // DH
    parts, cut = sums.shape[1], sums.shape[3]
    by_head = pl.BlockSpec((rows, DH), lambda h: (0, h))
    state = pl.BlockSpec((1, DH, DH), lambda h: (h, 0, 0))
    later = pl.BlockSpec((1, parts, 1, cut, DH), lambda h: (h, 0, 0, 0, 0))
    earlier = pl.BlockSpec((1, parts, 1, cut, DH), lambda h: (h, 0, 1, 0, 0))
    return pl.pallas_call(
        functools.partial(query_key_kernel, scaling),
        grid=(heads,),
        in_specs=[by_head] * 4 + [later, earlier, state, state],
        out_specs=[by_head, by_head],
        out_shape=[jax.ShapeDtypeStruct(q.shape, BF16)] * 2,
        compiler_params=params(),
        cost_estimate=QUICK,
        name="query_key_gradients",
    )(q, k, v, o, sums, sums, g, kv)


def x_spec(tokens, rows, at):
    return pl.BlockSpec((tokens, rows // 2), at)


def terms_kernel(scale, blocks, n_x, n_v, *refs):
    xs, vs, out_ref = refs[:n_x], refs[n_x : n_x + n_v], refs[n_x + n_v]
    piece = out_ref.shape[2]
    for n, (x, v) in enumerate(blocks):
        term = dot(xs[2 * x][...], vs[v][0], TN) + dot(xs[2 * x + 1][...], vs[v][1], TN)
        for low in range(2):
            out_ref[low, n] = (term[low * piece : (low + 1) * piece] * scale).astype(BF16)


def weight_terms(xs, vs, blocks, scale):
    tokens, rows = xs[0].shape
    cols = vs[0].shape[2]
    tail = (len(blocks), rows // 4, cols)
    return pl.pallas_call(
        functools.partial(terms_kernel, scale, blocks, len(xs), len(vs)),
        grid=(2,),
        in_specs=[x_spec(tokens, rows, lambda r: (0, r))] * len(xs)
        + [pl.BlockSpec((2, tokens, cols), lambda r: (0, 0, 0))] * len(vs),
        out_specs=pl.BlockSpec((2, *tail), lambda r: (r, 0, 0, 0)),
        out_shape=jax.ShapeDtypeStruct((4, *tail), BF16),
        compiler_params=params(),
        cost_estimate=QUICK,
        name="weight_terms",
    )(*xs, *vs)


def last_kernel(scale, at_ref, *refs):
    xs, v_ref, outs = refs[:4], refs[4], refs[5:]
    piece = outs[0].shape[0]
    for core, pair in enumerate((xs[2:], xs[:2])):

        @pl.when(at_ref[1] == core)
        def _(pair=pair):
            term = dot(pair[0][...], v_ref[0], TN) + dot(pair[1][...], v_ref[1], TN)
            for low in range(2):
                place = lax.rem(2 * pl.program_id(0) + low + 4 - at_ref[0], 4)
                rounded = (term[low * piece : (low + 1) * piece] * scale).astype(BF16)
                for d in range(4):

                    @pl.when(place == d)
                    def _(d=d, rounded=rounded):
                        outs[d][...] = rounded


def last_terms(at, xs, v, scale):
    tokens, rows = xs[0].shape
    cols = v.shape[2]
    shape = (rows // 4, cols)

    def used_by(core):
        return lambda r, s: (0, jnp.where(s[1] == core, r, 0))

    return pl.pallas_call(
        functools.partial(last_kernel, scale),
        grid_spec=pltpu.PrefetchScalarGridSpec(
            num_scalar_prefetch=1,
            grid=(2,),
            in_specs=[x_spec(tokens, rows, used_by(1))] * 2
            + [x_spec(tokens, rows, used_by(0))] * 2
            + [pl.BlockSpec((2, tokens, cols), lambda r, s: (0, 0, 0))],
            out_specs=[pl.BlockSpec(shape, lambda r, s: (0, 0))] * 4,
        ),
        out_shape=[jax.ShapeDtypeStruct(shape, BF16)] * 4,
        compiler_params=params(),
        cost_estimate=QUICK,
        name="last_terms",
    )(at, *xs, v)


def seq_index(x, y, c):
    return ((x % NX) * NY + (y % NY)) * NC + c


CHIPS = [(x, y, c) for x in range(NX) for y in range(NY) for c in range(NC)]
SWAP = [(seq_index(x, y, c), seq_index(x, y, 1 - c)) for x, y, c in CHIPS]


def shift(axis, d):
    dx, dy = (d, 0) if axis == "x" else (0, d)
    return [(seq_index(x, y, c), seq_index(x + dx, y + dy, c)) for x, y, c in CHIPS]


def shift_to(axis, targets, d):
    at = {seq_index(x, y, c): (x if axis == "x" else y) for x, y, c in CHIPS}
    return [(a, b) for a, b in shift(axis, d) if at[b] in targets]


def total(parts):
    acc = parts[0].astype(F32)
    for part in parts[1:]:
        acc = acc + part.astype(F32)
    return acc.astype(BF16)


def send_all(axis, sums):
    return [lax.ppermute(sums[d], "seq", shift(axis, d)) for d in (2, 1, 3)]


def choose(pieces, targets, at):
    chosen = []
    for d in range(4):
        piece = pieces[0]
        for t, other in zip(targets[1:], pieces[1:]):
            piece = jnp.where(at == (t - d) % 4, other, piece)
        chosen.append(piece)
    return chosen


def send_to(axis, chosen, targets):
    return [lax.ppermute(chosen[d], "seq", shift_to(axis, targets, d)) for d in (2, 1, 3)]


HELD_AT_X = ((2, 1), (-2, -1), (3, 2), (-3, -2))
HELD_AT_Y = ((0, 0), (1, 0), (-1, 0), (4, None))
LAST = 3
LAST_STEP = (-3, 3)


def to_x(d, nz):
    return [
        (seq_index(x, y, c) * nz + m, seq_index(x + d, y, c) * nz + (m + HELD_AT_X[(x + d) % NX][1]) % nz)
        for x, y, c in CHIPS
        for m in range(nz)
    ]


def to_last(d, nz):
    return [
        (seq_index(x, y, c) * nz + m, seq_index(x, LAST, c) * nz + (m + LAST_STEP[c]) % nz)
        for x, y, c in CHIPS
        for m in range(nz)
        if (y + d) % NY == LAST
    ]


def owners(turn, nz):
    pairs = []
    for x, y, c in CHIPS:
        by_x = c == turn
        r = y if by_x else x
        d = HELD_AT_X[x][0] if by_x else HELD_AT_Y[y][0]
        for j in range(nz):
            pairs.append((seq_index(x, y, c) * nz + j, (4 * ((j - d) % nz) + r) * nz + j))
    return pairs


def per_device(layer_input, queries, keys, values, out_grad):
    tok_rows, features = queries.shape
    half = features // 2
    n_seq, n_z = lax.axis_size("seq"), lax.axis_size("head")
    scaling = 1.0 / math.sqrt(DH * tok_rows * n_seq)
    weight_scale = 1.0 / math.sqrt(tok_rows * n_seq)
    s = lax.axis_index("seq").astype(jnp.int32)
    z = lax.axis_index("head").astype(jnp.int32)
    x, y, c = s // (NY * NC), lax.rem(s // NC, NY), lax.rem(s, NC)
    core, at_x = c.reshape(1), jnp.stack([x, c])
    up = [(i, (i + 1) % n_z) for i in range(n_z)]
    down = [(i, (i - 1) % n_z) for i in range(n_z)]
    both = ("seq", "head")
    apart = [
        (seq_index(a, b, e) * n_z + m, seq_index(a, b, e) * n_z + (m + 1 - 2 * e) % n_z)
        for a, b, e in CHIPS
        for m in range(n_z)
    ]

    def go(array, way):
        return lax.ppermute(array, "head", way)

    def swap(array):
        return lax.ppermute(array, "seq", SWAP)

    def terms(xs, vs, blocks):
        return weight_terms(xs, vs, blocks, weight_scale)

    groups = {
        "x": [[seq_index(a, b, e) for a in range(NX)] for b in range(NY) for e in range(NC)],
        "y": [[seq_index(a, b, e) for b in range(NY)] for a in range(NX) for e in range(NC)],
    }

    def exchange(axis, pieces):
        return lax.all_to_all(pieces, "seq", 0, 0, axis_index_groups=groups[axis])

    prev0, next0 = go(layer_input, up), go(layer_input, down)
    kv0, g1, totals, packed = local_states(core, queries, keys, values, out_grad, n_seq)
    spread = lax.all_to_all(totals.reshape(n_seq, *totals.shape[2:]), "seq", 0, 0)
    sums = lax.all_to_all(running_sums(spread), "seq", 0, 0)
    sums = sums.reshape(*totals.shape[:2], *sums.shape[1:])
    packed = swap(packed)
    v0 = value_gradient(core, queries, keys, out_grad, packed, sums, scaling)

    u1, d1 = go(v0, up), go(v0, down)
    prev0, next0, kv0, x_own, _ = tie(prev0, next0, kv0, layer_input, v0)
    prev1, next1, own1 = swap(prev0), swap(next0), swap(x_own)
    near = [prev0, prev1, next0, next1]
    t0 = terms([x_own, own1, *near], [v0], [(0, 0), (1, 0), (2, 0)])

    p0 = exchange("x", t0)
    kv0 = tie(kv0, t0)[0]
    query_grad, key_grad = query_key_gradients(queries, keys, values, out_grad, sums, g1, kv0, scaling)

    u1, d1, query_grad, key_grad = tie(u1, d1, query_grad, key_grad)
    u2, d2 = go(u1, up), go(d1, down)
    t1 = terms(near, [d1, u1], [(0, 0), (1, 1)])
    p0 = total(list(tie(p0, t1)[0]))
    p1 = exchange("y", t1)
    c0 = choose([p0[0], p0[1], p0[2]], [0, 1, 2], y)
    y0 = send_to("y", c0, [0, 1, 2])

    u2, d2, *y0 = tie(u2, d2, *y0, t1)[:5]
    v3 = lax.ppermute(jnp.where(c == 0, u2, d2), both, apart)
    t2 = terms(near, [d2, u2], [(0, 0), (1, 1)])
    p1 = total(list(p1))
    p2 = exchange("y", t2)

    v3, p1, r0 = tie(v3, p1, total([c0[0]] + y0), t2)[:3]
    q3 = last_terms(at_x, near, v3, weight_scale)
    x3 = send_all("x", q3)
    p2 = total(list(tie(p2, q3[0])[0]))
    held = choose([p1[0], p1[1], p2[0], p2[1]], [0, 1, 2, 3], x)
    x2 = [lax.ppermute(held[d], both, to_x(d, n_z)) for d in (0, 2, 1, 3)]
    p3 = total([q3[0]] + x3)

    p3 = tie(p3, *held)[0]
    y3 = [lax.ppermute(p3, both, to_last(d, n_z)) for d in (0, 2, 1, 3)]
    held_x = total(x2)
    first = jnp.where(c == 0, held_x, r0)
    second = jnp.where(c == 0, r0, held_x)
    r3 = total(y3)
    last = y == LAST
    first = jnp.where((c == 1) & last, r3, first)
    second = jnp.where((c == 0) & last, r3, second)
    first = lax.ppermute(first, both, owners(0, n_z))
    second = lax.ppermute(second, both, owners(1, n_z))

    away = lax.rem(z - s // 4 + n_z, n_z)
    by_x = (away == 2) | (away == 3) | (away == 5) | (away == 6)
    left = jnp.where(by_x, first, second)
    right = jnp.where(by_x, second, first)
    weight_grad = jnp.concatenate([left, right], 1).astype(F32)
    return (query_grad, key_grad, weight_grad)


def solution(mesh):
    return jax.shard_map(
        per_device,
        mesh=mesh,
        in_specs=(P("seq", "head"),) * 5,
        out_specs=(P("seq", "head"),) * 3,
        check_vma=False,
    )
```

```python
import functools
import math

import jax
import jax.numpy as jnp
from jax import lax
from jax.experimental import pallas as pl
from jax.experimental.pallas import tpu as pltpu
from jax.sharding import PartitionSpec as P

DH = 128
BLOCK = 512
HALF = BLOCK // 2
NX, NY, NC = 4, 4, 2
BF16 = jnp.bfloat16
F32 = jnp.float32

NN = (((1,), (0,)), ((), ()))
NT = (((1,), (1,)), ((), ()))
TN = (((0,), (0,)), ((), ()))


def dot(a, b, dims):
    return lax.dot_general(a, b, dims, preferred_element_type=F32)


QUICK = pl.CostEstimate(flops=1, bytes_accessed=1, transcendentals=0)


def params(mib=58):
    return pltpu.CompilerParams(vmem_limit_bytes=mib * 1024 * 1024)


def tie(*arrays):
    return lax.optimization_barrier(arrays)


def states_kernel(_, q_ref, k_ref, v_ref, o_ref, kv_ref, g_ref, tot_ref, pack_ref):
    kv = []
    g = []
    for b in range(2):
        rows = pl.ds(b * BLOCK, BLOCK)
        kv.append(dot(k_ref[rows, :], v_ref[rows, :], TN))
        g.append(dot(q_ref[rows, :], o_ref[rows, :], TN))
    kv_ref[0] = kv[0]
    g_ref[0] = g[1]
    cut = tot_ref.shape[3]
    for p in range(DH // cut):
        rows = slice(p * cut, (p + 1) * cut)
        tot_ref[0, p, 0] = (g[0] + g[1])[rows].astype(BF16)
        tot_ref[0, p, 1] = (kv[0] + kv[1])[rows].astype(BF16)

    @pl.when(pl.program_id(0) < 2)
    def _():
        for p, ref in enumerate((q_ref, k_ref, o_ref)):
            pack_ref[p] = ref[...]


def local_states(core, q, k, v, o, n_seq):
    rows, features = q.shape
    heads = features // DH
    parts = n_seq // heads

    def head(h, c):
        return lax.rem(2 * (1 - c[0]) + h, heads)

    by_head = pl.BlockSpec((rows, DH), lambda h, c: (0, head(h, c)))
    state = pl.BlockSpec((1, DH, DH), lambda h, c: (head(h, c), 0, 0))
    cuts = (parts, 2, DH // parts, DH)
    return pl.pallas_call(
        states_kernel,
        grid_spec=pltpu.PrefetchScalarGridSpec(
            num_scalar_prefetch=1,
            grid=(heads,),
            in_specs=[by_head] * 4,
            out_specs=[
                state,
                state,
                pl.BlockSpec((1, *cuts), lambda h, c: (head(h, c), 0, 0, 0, 0)),
                pl.BlockSpec((3, rows, DH), lambda h, c: (0, 0, jnp.minimum(h, 1))),
            ],
        ),
        out_shape=[
            jax.ShapeDtypeStruct((heads, DH, DH), F32),
            jax.ShapeDtypeStruct((heads, DH, DH), F32),
            jax.ShapeDtypeStruct((heads, *cuts), BF16),
            jax.ShapeDtypeStruct((3, rows, 2 * DH), BF16),
        ],
        compiler_params=params(),
        cost_estimate=QUICK,
        name="states",
    )(core, q, k, v, o)


def sums_kernel(in_ref, out_ref):
    n = in_ref.shape[0]
    for which, order in ((0, range(n - 1, -1, -1)), (1, range(n))):
        acc = jnp.zeros(in_ref.shape[2:], F32)
        for at in order:
            part = acc.astype(BF16)
            out_ref[at, which] = part
            if which == 0:
                out_ref[at ^ 1, 2] = part
            acc = acc + in_ref[at, which].astype(F32)


def running_sums(parts):
    return pl.pallas_call(
        sums_kernel,
        out_shape=jax.ShapeDtypeStruct((parts.shape[0], 3, *parts.shape[2:]), BF16),
        compiler_params=params(),
        cost_estimate=QUICK,
        name="running_sums",
    )(parts)


def keep(s0, t0, rows, cols, upper):
    s = lax.broadcasted_iota(jnp.int32, (rows, cols), 0) + s0
    t = lax.broadcasted_iota(jnp.int32, (rows, cols), 1) + t0
    return t >= s if upper else t <= s


def upper_product(a, b, c):
    top = dot(a[:HALF], b, NT)
    top = jnp.where(keep(0, 0, HALF, BLOCK, True), top, 0.0).astype(BF16)
    low = dot(a[HALF:], b[HALF:], NT)
    low = jnp.where(keep(0, 0, HALF, HALF, True), low, 0.0).astype(BF16)
    return jnp.concatenate([dot(top, c, NN), dot(low, c[HALF:], NN)], 0)


def lower_product(a, b, c):
    top = dot(a[:HALF], b[:HALF], NT)
    top = jnp.where(keep(0, 0, HALF, HALF, False), top, 0.0).astype(BF16)
    low = dot(a[HALF:], b, NT)
    low = jnp.where(keep(HALF, 0, HALF, BLOCK, False), low, 0.0).astype(BF16)
    return jnp.concatenate([dot(top, c[:HALF], NN), dot(low, c, NN)], 0)


def value_kernel(scaling, _, *refs):
    own, other = refs[:3], refs[3:6]
    own_later, other_later, out_ref = refs[6:]

    def load(members, b):
        rows = pl.ds(b * BLOCK, BLOCK)
        return [ref[rows, :] if len(ref.shape) == 2 else ref[0, rows, :] for ref in members]

    for at, (members, later) in enumerate(((own, own_later), (other, other_later))):
        after = later[0, :, 0].reshape(DH, DH).astype(F32)
        for b in (1, 0):
            q, k, o = load(members, b)
            grad = upper_product(k, q, o) + dot(k, after.astype(BF16), NN)
            out_ref[at, pl.ds(b * BLOCK, BLOCK), :] = (grad * scaling).astype(BF16)
            if b == 1:
                after = after + dot(q, o, TN)


def value_gradient(core, q, k, o, packed, sums, scaling):
    rows = q.shape[0]
    parts, cut = sums.shape[1], sums.shape[3]
    own = pl.BlockSpec((rows, DH), lambda h, c: (0, 2 * c[0] + h))
    other = [pl.BlockSpec((1, rows, DH), lambda h, c, p=p: (p, 0, h)) for p in range(3)]
    later = [
        pl.BlockSpec((1, parts, 1, cut, DH), lambda h, c, k=k: (2 * c[0] + h, 0, k, 0, 0)) for k in (0, 2)
    ]
    out = pl.BlockSpec((2, rows, DH), lambda h, c: (0, 0, h))
    return pl.pallas_call(
        functools.partial(value_kernel, scaling),
        grid_spec=pltpu.PrefetchScalarGridSpec(
            num_scalar_prefetch=1,
            grid=(2,),
            in_specs=[own] * 3 + other + later,
            out_specs=out,
        ),
        out_shape=jax.ShapeDtypeStruct((2, rows, 2 * DH), BF16),
        compiler_params=params(52),
        cost_estimate=QUICK,
        name="value_gradient",
    )(core, q, k, o, packed, packed, packed, sums, sums)


def query_key_kernel(scaling, q_ref, k_ref, v_ref, o_ref, later_ref, before_ref, g_ref, kv_ref, dq_ref, dk_ref):
    later = later_ref[0, :, 0].reshape(DH, DH).astype(F32)
    earlier = before_ref[0, :, 0].reshape(DH, DH).astype(F32)
    for b in range(2):
        rows = pl.ds(b * BLOCK, BLOCK)
        q, k, v, o = q_ref[rows, :], k_ref[rows, :], v_ref[rows, :], o_ref[rows, :]
        after = (later + g_ref[0]) if b == 0 else later
        before = earlier if b == 0 else (earlier + kv_ref[0])
        dq = lower_product(o, v, k) + dot(o, before.astype(BF16), NT)
        dk = upper_product(v, o, q) + dot(v, after.astype(BF16), NT)
        dq_ref[rows, :] = (dq * scaling).astype(BF16)
        dk_ref[rows, :] = (dk * scaling).astype(BF16)


def query_key_gradients(q, k, v, o, sums, g, kv, scaling):
    rows = q.shape[0]
    heads = q.shape[1] // DH
    parts, cut = sums.shape[1], sums.shape[3]
    by_head = pl.BlockSpec((rows, DH), lambda h: (0, h))
    state = pl.BlockSpec((1, DH, DH), lambda h: (h, 0, 0))
    later = pl.BlockSpec((1, parts, 1, cut, DH), lambda h: (h, 0, 0, 0, 0))
    earlier = pl.BlockSpec((1, parts, 1, cut, DH), lambda h: (h, 0, 1, 0, 0))
    return pl.pallas_call(
        functools.partial(query_key_kernel, scaling),
        grid=(heads,),
        in_specs=[by_head] * 4 + [later, earlier, state, state],
        out_specs=[by_head, by_head],
        out_shape=[jax.ShapeDtypeStruct(q.shape, BF16)] * 2,
        compiler_params=params(),
        cost_estimate=QUICK,
        name="query_key_gradients",
    )(q, k, v, o, sums, sums, g, kv)


def x_spec(tokens, rows, at):
    return pl.BlockSpec((tokens, rows // 2), at)


def terms_kernel(scale, blocks, n_x, n_v, *refs):
    xs, vs, out_ref = refs[:n_x], refs[n_x : n_x + n_v], refs[n_x + n_v]
    piece = out_ref.shape[2]
    for n, (x, v) in enumerate(blocks):
        term = dot(xs[2 * x][...], vs[v][0], TN) + dot(xs[2 * x + 1][...], vs[v][1], TN)
        for low in range(2):
            out_ref[low, n] = (term[low * piece : (low + 1) * piece] * scale).astype(BF16)


def weight_terms(xs, vs, blocks, scale):
    tokens, rows = xs[0].shape
    cols = vs[0].shape[2]
    tail = (len(blocks), rows // 4, cols)
    return pl.pallas_call(
        functools.partial(terms_kernel, scale, blocks, len(xs), len(vs)),
        grid=(2,),
        in_specs=[x_spec(tokens, rows, lambda r: (0, r))] * len(xs)
        + [pl.BlockSpec((2, tokens, cols), lambda r: (0, 0, 0))] * len(vs),
        out_specs=pl.BlockSpec((2, *tail), lambda r: (r, 0, 0, 0)),
        out_shape=jax.ShapeDtypeStruct((4, *tail), BF16),
        compiler_params=params(),
        cost_estimate=QUICK,
        name="weight_terms",
    )(*xs, *vs)


def last_kernel(scale, at_ref, *refs):
    xs, v_ref, outs = refs[:4], refs[4], refs[5:]
    piece = outs[0].shape[0]
    for core, pair in enumerate((xs[2:], xs[:2])):

        @pl.when(at_ref[1] == core)
        def _(pair=pair):
            term = dot(pair[0][...], v_ref[0], TN) + dot(pair[1][...], v_ref[1], TN)
            for low in range(2):
                place = lax.rem(2 * pl.program_id(0) + low + 4 - at_ref[0], 4)
                rounded = (term[low * piece : (low + 1) * piece] * scale).astype(BF16)
                for d in range(4):

                    @pl.when(place == d)
                    def _(d=d, rounded=rounded):
                        outs[d][...] = rounded


def last_terms(at, xs, v, scale):
    tokens, rows = xs[0].shape
    cols = v.shape[2]
    shape = (rows // 4, cols)

    def used_by(core):
        return lambda r, s: (0, jnp.where(s[1] == core, r, 0))

    return pl.pallas_call(
        functools.partial(last_kernel, scale),
        grid_spec=pltpu.PrefetchScalarGridSpec(
            num_scalar_prefetch=1,
            grid=(2,),
            in_specs=[x_spec(tokens, rows, used_by(1))] * 2
            + [x_spec(tokens, rows, used_by(0))] * 2
            + [pl.BlockSpec((2, tokens, cols), lambda r, s: (0, 0, 0))],
            out_specs=[pl.BlockSpec(shape, lambda r, s: (0, 0))] * 4,
        ),
        out_shape=[jax.ShapeDtypeStruct(shape, BF16)] * 4,
        compiler_params=params(),
        cost_estimate=QUICK,
        name="last_terms",
    )(at, *xs, v)


def seq_index(x, y, c):
    return ((x % NX) * NY + (y % NY)) * NC + c


CHIPS = [(x, y, c) for x in range(NX) for y in range(NY) for c in range(NC)]
SWAP = [(seq_index(x, y, c), seq_index(x, y, 1 - c)) for x, y, c in CHIPS]


def shift(axis, d):
    dx, dy = (d, 0) if axis == "x" else (0, d)
    return [(seq_index(x, y, c), seq_index(x + dx, y + dy, c)) for x, y, c in CHIPS]


def shift_to(axis, targets, d):
    at = {seq_index(x, y, c): (x if axis == "x" else y) for x, y, c in CHIPS}
    return [(a, b) for a, b in shift(axis, d) if at[b] in targets]


def total(parts):
    acc = parts[0].astype(F32)
    for part in parts[1:]:
        acc = acc + part.astype(F32)
    return acc.astype(BF16)


def send_all(axis, sums):
    return [lax.ppermute(sums[d], "seq", shift(axis, d)) for d in (2, 1, 3)]


def choose(pieces, targets, at):
    chosen = []
    for d in range(4):
        piece = pieces[0]
        for t, other in zip(targets[1:], pieces[1:]):
            piece = jnp.where(at == (t - d) % 4, other, piece)
        chosen.append(piece)
    return chosen


def send_to(axis, chosen, targets):
    return [lax.ppermute(chosen[d], "seq", shift_to(axis, targets, d)) for d in (2, 1, 3)]


HELD_AT_X = ((2, 1), (-2, -1), (3, 2), (-3, -2))
HELD_AT_Y = ((0, 0), (1, 0), (-1, 0), (4, None))
LAST = 3
LAST_STEP = (-3, 3)


def to_last(d):
    return [(a, b) for (x, y, c), (a, b) in zip(CHIPS, shift("y", d)) if (y + d) % NY == LAST]


def owners(turn, nz):
    pairs = []
    for x, y, c in CHIPS:
        by_x = c == turn
        r = y if by_x else x
        d = HELD_AT_X[x][0] if by_x else HELD_AT_Y[y][0]
        step = HELD_AT_X[x][1] if by_x else LAST_STEP[c] if y == LAST else 0
        for m in range(nz):
            j = (m + step) % nz
            pairs.append((seq_index(x, y, c) * nz + m, (4 * ((j - d) % nz) + r) * nz + j))
    return pairs


def per_device(layer_input, queries, keys, values, out_grad):
    tok_rows, features = queries.shape
    half = features // 2
    n_seq, n_z = lax.axis_size("seq"), lax.axis_size("head")
    scaling = 1.0 / math.sqrt(DH * tok_rows * n_seq)
    weight_scale = 1.0 / math.sqrt(tok_rows * n_seq)
    s = lax.axis_index("seq").astype(jnp.int32)
    z = lax.axis_index("head").astype(jnp.int32)
    x, y, c = s // (NY * NC), lax.rem(s // NC, NY), lax.rem(s, NC)
    core, at_x = c.reshape(1), jnp.stack([x, c])
    up = [(i, (i + 1) % n_z) for i in range(n_z)]
    down = [(i, (i - 1) % n_z) for i in range(n_z)]
    both = ("seq", "head")
    apart = [
        (seq_index(a, b, e) * n_z + m, seq_index(a, b, e) * n_z + (m + 1 - 2 * e) % n_z)
        for a, b, e in CHIPS
        for m in range(n_z)
    ]

    def go(array, way):
        return lax.ppermute(array, "head", way)

    def swap(array):
        return lax.ppermute(array, "seq", SWAP)

    def terms(xs, vs, blocks):
        return weight_terms(xs, vs, blocks, weight_scale)

    groups = {
        "x": [[seq_index(a, b, e) for a in range(NX)] for b in range(NY) for e in range(NC)],
        "y": [[seq_index(a, b, e) for b in range(NY)] for a in range(NX) for e in range(NC)],
    }

    def exchange(axis, pieces):
        return lax.all_to_all(pieces, "seq", 0, 0, axis_index_groups=groups[axis])

    prev0, next0 = go(layer_input, up), go(layer_input, down)
    kv0, g1, totals, packed = local_states(core, queries, keys, values, out_grad, n_seq)
    spread = lax.all_to_all(totals.reshape(n_seq, *totals.shape[2:]), "seq", 0, 0)
    sums = lax.all_to_all(running_sums(spread), "seq", 0, 0)
    sums = sums.reshape(*totals.shape[:2], *sums.shape[1:])
    packed = swap(packed)
    v0 = value_gradient(core, queries, keys, out_grad, packed, sums, scaling)

    u1, d1 = go(v0, up), go(v0, down)
    prev0, next0, kv0, x_own, _ = tie(prev0, next0, kv0, layer_input, v0)
    prev1, next1, own1 = swap(prev0), swap(next0), swap(x_own)
    near = [prev0, prev1, next0, next1]
    t0 = terms([x_own, own1, *near], [v0], [(0, 0), (1, 0), (2, 0)])

    p0 = exchange("x", t0)
    kv0 = tie(kv0, t0)[0]
    query_grad, key_grad = query_key_gradients(queries, keys, values, out_grad, sums, g1, kv0, scaling)

    u1, d1, query_grad, key_grad = tie(u1, d1, query_grad, key_grad)
    u2, d2 = go(u1, up), go(d1, down)
    t1 = terms(near, [d1, u1], [(0, 0), (1, 1)])
    p0 = total(list(tie(p0, t1)[0]))
    p1 = exchange("y", t1)
    c0 = choose([p0[0], p0[1], p0[2]], [0, 1, 2], y)
    y0 = send_to("y", c0, [0, 1, 2])

    u2, d2, *y0 = tie(u2, d2, *y0, t1)[:5]
    v3 = lax.ppermute(jnp.where(c == 0, u2, d2), both, apart)
    t2 = terms(near, [d2, u2], [(0, 0), (1, 1)])
    p1 = total(list(p1))
    p2 = exchange("y", t2)

    v3, p1, r0 = tie(v3, p1, total([c0[0]] + y0), t2)[:3]
    q3 = last_terms(at_x, near, v3, weight_scale)
    x3 = send_all("x", q3)
    p2 = total(list(tie(p2, q3[0])[0]))
    held = choose([p1[0], p1[1], p2[0], p2[1]], [0, 1, 2, 3], x)
    x2 = [held[0]] + send_all("x", held)
    p3 = total([q3[0]] + x3)

    p3 = tie(p3, *held)[0]
    y3 = [p3] + [lax.ppermute(p3, "seq", to_last(d)) for d in (2, 1, 3)]
    held_x = total(x2)
    first = jnp.where(c == 0, held_x, r0)
    second = jnp.where(c == 0, r0, held_x)
    r3 = total(y3)
    last = y == LAST
    first = jnp.where((c == 1) & last, r3, first)
    second = jnp.where((c == 0) & last, r3, second)
    first = lax.ppermute(first, both, owners(0, n_z))
    second = lax.ppermute(second, both, owners(1, n_z))

    away = lax.rem(z - s // 4 + n_z, n_z)
    by_x = (away == 2) | (away == 3) | (away == 5) | (away == 6)
    left = jnp.where(by_x, first, second)
    right = jnp.where(by_x, second, first)
    weight_grad = jnp.concatenate([left, right], 1).astype(F32)
    return (query_grad, key_grad, weight_grad)


def solution(mesh):
    return jax.shard_map(
        per_device,
        mesh=mesh,
        in_specs=(P("seq", "head"),) * 5,
        out_specs=(P("seq", "head"),) * 3,
        check_vma=False,
    )
```

```python
import functools
import math

import jax
import jax.numpy as jnp
from jax import lax
from jax.experimental import pallas as pl
from jax.experimental.pallas import tpu as pltpu
from jax.sharding import PartitionSpec as P

DH = 128
BLOCK = 512
HALF = BLOCK // 2
NX, NY, NC = 4, 4, 2
BF16 = jnp.bfloat16
F32 = jnp.float32

NN = (((1,), (0,)), ((), ()))
NT = (((1,), (1,)), ((), ()))
TN = (((0,), (0,)), ((), ()))


def dot(a, b, dims):
    return lax.dot_general(a, b, dims, preferred_element_type=F32)


QUICK = pl.CostEstimate(flops=1, bytes_accessed=1, transcendentals=0)


def params(mib=58):
    return pltpu.CompilerParams(vmem_limit_bytes=mib * 1024 * 1024)


def tie(*arrays):
    return lax.optimization_barrier(arrays)


def states_kernel(_, q_ref, k_ref, v_ref, o_ref, kv_ref, g_ref, tot_ref, pack_ref):
    kv = []
    g = []
    for b in range(2):
        rows = pl.ds(b * BLOCK, BLOCK)
        kv.append(dot(k_ref[rows, :], v_ref[rows, :], TN))
        g.append(dot(q_ref[rows, :], o_ref[rows, :], TN))
    kv_ref[0] = kv[0]
    g_ref[0] = g[1]
    cut = tot_ref.shape[3]
    for p in range(DH // cut):
        rows = slice(p * cut, (p + 1) * cut)
        tot_ref[0, p, 0] = (g[0] + g[1])[rows].astype(BF16)
        tot_ref[0, p, 1] = (kv[0] + kv[1])[rows].astype(BF16)

    @pl.when(pl.program_id(0) < 2)
    def _():
        for p, ref in enumerate((q_ref, k_ref, o_ref)):
            pack_ref[p] = ref[...]


def local_states(core, q, k, v, o, n_seq):
    rows, features = q.shape
    heads = features // DH
    parts = n_seq // heads

    def head(h, c):
        return lax.rem(2 * (1 - c[0]) + h, heads)

    by_head = pl.BlockSpec((rows, DH), lambda h, c: (0, head(h, c)))
    state = pl.BlockSpec((1, DH, DH), lambda h, c: (head(h, c), 0, 0))
    cuts = (parts, 2, DH // parts, DH)
    return pl.pallas_call(
        states_kernel,
        grid_spec=pltpu.PrefetchScalarGridSpec(
            num_scalar_prefetch=1,
            grid=(heads,),
            in_specs=[by_head] * 4,
            out_specs=[
                state,
                state,
                pl.BlockSpec((1, *cuts), lambda h, c: (head(h, c), 0, 0, 0, 0)),
                pl.BlockSpec((3, rows, DH), lambda h, c: (0, 0, jnp.minimum(h, 1))),
            ],
        ),
        out_shape=[
            jax.ShapeDtypeStruct((heads, DH, DH), F32),
            jax.ShapeDtypeStruct((heads, DH, DH), F32),
            jax.ShapeDtypeStruct((heads, *cuts), BF16),
            jax.ShapeDtypeStruct((3, rows, 2 * DH), BF16),
        ],
        compiler_params=params(),
        cost_estimate=QUICK,
        name="states",
    )(core, q, k, v, o)


def sums_kernel(in_ref, out_ref):
    n = in_ref.shape[0]
    for which, order in ((0, range(n - 1, -1, -1)), (1, range(n))):
        acc = jnp.zeros(in_ref.shape[2:], F32)
        for at in order:
            part = acc.astype(BF16)
            out_ref[at, which] = part
            if which == 0:
                out_ref[at ^ 1, 2] = part
            acc = acc + in_ref[at, which].astype(F32)


def running_sums(parts):
    return pl.pallas_call(
        sums_kernel,
        out_shape=jax.ShapeDtypeStruct((parts.shape[0], 3, *parts.shape[2:]), BF16),
        compiler_params=params(),
        cost_estimate=QUICK,
        name="running_sums",
    )(parts)


def keep(s0, t0, rows, cols, upper):
    s = lax.broadcasted_iota(jnp.int32, (rows, cols), 0) + s0
    t = lax.broadcasted_iota(jnp.int32, (rows, cols), 1) + t0
    return t >= s if upper else t <= s


def upper_product(a, b, c):
    top = dot(a[:HALF], b, NT)
    top = jnp.where(keep(0, 0, HALF, BLOCK, True), top, 0.0).astype(BF16)
    low = dot(a[HALF:], b[HALF:], NT)
    low = jnp.where(keep(0, 0, HALF, HALF, True), low, 0.0).astype(BF16)
    return jnp.concatenate([dot(top, c, NN), dot(low, c[HALF:], NN)], 0)


def lower_product(a, b, c):
    top = dot(a[:HALF], b[:HALF], NT)
    top = jnp.where(keep(0, 0, HALF, HALF, False), top, 0.0).astype(BF16)
    low = dot(a[HALF:], b, NT)
    low = jnp.where(keep(HALF, 0, HALF, BLOCK, False), low, 0.0).astype(BF16)
    return jnp.concatenate([dot(top, c[:HALF], NN), dot(low, c, NN)], 0)


def value_kernel(scaling, _, *refs):
    own, other = refs[:3], refs[3:6]
    own_later, other_later, out_ref = refs[6:]

    def load(members, b):
        rows = pl.ds(b * BLOCK, BLOCK)
        return [ref[rows, :] if len(ref.shape) == 2 else ref[0, rows, :] for ref in members]

    for at, (members, later) in enumerate(((own, own_later), (other, other_later))):
        after = later[0, :, 0].reshape(DH, DH).astype(F32)
        for b in (1, 0):
            q, k, o = load(members, b)
            grad = upper_product(k, q, o) + dot(k, after.astype(BF16), NN)
            out_ref[at, pl.ds(b * BLOCK, BLOCK), :] = (grad * scaling).astype(BF16)
            if b == 1:
                after = after + dot(q, o, TN)


def value_gradient(core, q, k, o, packed, sums, scaling):
    rows = q.shape[0]
    parts, cut = sums.shape[1], sums.shape[3]
    own = pl.BlockSpec((rows, DH), lambda h, c: (0, 2 * c[0] + h))
    other = [pl.BlockSpec((1, rows, DH), lambda h, c, p=p: (p, 0, h)) for p in range(3)]
    later = [
        pl.BlockSpec((1, parts, 1, cut, DH), lambda h, c, k=k: (2 * c[0] + h, 0, k, 0, 0)) for k in (0, 2)
    ]
    out = pl.BlockSpec((2, rows, DH), lambda h, c: (0, 0, h))
    return pl.pallas_call(
        functools.partial(value_kernel, scaling),
        grid_spec=pltpu.PrefetchScalarGridSpec(
            num_scalar_prefetch=1,
            grid=(2,),
            in_specs=[own] * 3 + other + later,
            out_specs=out,
        ),
        out_shape=jax.ShapeDtypeStruct((2, rows, 2 * DH), BF16),
        compiler_params=params(52),
        cost_estimate=QUICK,
        name="value_gradient",
    )(core, q, k, o, packed, packed, packed, sums, sums)


def query_key_kernel(scaling, q_ref, k_ref, v_ref, o_ref, later_ref, before_ref, g_ref, kv_ref, dq_ref, dk_ref):
    later = later_ref[0, :, 0].reshape(DH, DH).astype(F32)
    earlier = before_ref[0, :, 0].reshape(DH, DH).astype(F32)
    for b in range(2):
        rows = pl.ds(b * BLOCK, BLOCK)
        q, k, v, o = q_ref[rows, :], k_ref[rows, :], v_ref[rows, :], o_ref[rows, :]
        after = (later + g_ref[0]) if b == 0 else later
        before = earlier if b == 0 else (earlier + kv_ref[0])
        dq = lower_product(o, v, k) + dot(o, before.astype(BF16), NT)
        dk = upper_product(v, o, q) + dot(v, after.astype(BF16), NT)
        dq_ref[rows, :] = (dq * scaling).astype(BF16)
        dk_ref[rows, :] = (dk * scaling).astype(BF16)


def query_key_gradients(q, k, v, o, sums, g, kv, scaling):
    rows = q.shape[0]
    heads = q.shape[1] // DH
    parts, cut = sums.shape[1], sums.shape[3]
    by_head = pl.BlockSpec((rows, DH), lambda h: (0, h))
    state = pl.BlockSpec((1, DH, DH), lambda h: (h, 0, 0))
    later = pl.BlockSpec((1, parts, 1, cut, DH), lambda h: (h, 0, 0, 0, 0))
    earlier = pl.BlockSpec((1, parts, 1, cut, DH), lambda h: (h, 0, 1, 0, 0))
    return pl.pallas_call(
        functools.partial(query_key_kernel, scaling),
        grid=(heads,),
        in_specs=[by_head] * 4 + [later, earlier, state, state],
        out_specs=[by_head, by_head],
        out_shape=[jax.ShapeDtypeStruct(q.shape, BF16)] * 2,
        compiler_params=params(),
        cost_estimate=QUICK,
        name="query_key_gradients",
    )(q, k, v, o, sums, sums, g, kv)


def x_spec(tokens, rows, at):
    return pl.BlockSpec((tokens, rows // 2), at)


def terms_kernel(scale, blocks, n_x, n_v, *refs):
    xs, vs, out_ref = refs[:n_x], refs[n_x : n_x + n_v], refs[n_x + n_v]
    piece = out_ref.shape[2]
    for n, (x, v) in enumerate(blocks):
        term = dot(xs[2 * x][...], vs[v][0], TN) + dot(xs[2 * x + 1][...], vs[v][1], TN)
        for low in range(2):
            out_ref[low, n] = (term[low * piece : (low + 1) * piece] * scale).astype(BF16)


def weight_terms(xs, vs, blocks, scale):
    tokens, rows = xs[0].shape
    cols = vs[0].shape[2]
    tail = (len(blocks), rows // 4, cols)
    return pl.pallas_call(
        functools.partial(terms_kernel, scale, blocks, len(xs), len(vs)),
        grid=(2,),
        in_specs=[x_spec(tokens, rows, lambda r: (0, r))] * len(xs)
        + [pl.BlockSpec((2, tokens, cols), lambda r: (0, 0, 0))] * len(vs),
        out_specs=pl.BlockSpec((2, *tail), lambda r: (r, 0, 0, 0)),
        out_shape=jax.ShapeDtypeStruct((4, *tail), BF16),
        compiler_params=params(),
        cost_estimate=QUICK,
        name="weight_terms",
    )(*xs, *vs)


def last_kernel(scale, at_ref, *refs):
    xs, v_ref, outs = refs[:4], refs[4], refs[5:]
    piece = outs[0].shape[0]
    for core, pair in enumerate((xs[2:], xs[:2])):

        @pl.when(at_ref[1] == core)
        def _(pair=pair):
            term = dot(pair[0][...], v_ref[0], TN) + dot(pair[1][...], v_ref[1], TN)
            for low in range(2):
                place = lax.rem(2 * pl.program_id(0) + low + 4 - at_ref[0], 4)
                rounded = (term[low * piece : (low + 1) * piece] * scale).astype(BF16)
                for d in range(4):

                    @pl.when(place == d)
                    def _(d=d, rounded=rounded):
                        outs[d][...] = rounded


def last_terms(at, xs, v, scale):
    tokens, rows = xs[0].shape
    cols = v.shape[2]
    shape = (rows // 4, cols)

    def used_by(core):
        return lambda r, s: (0, jnp.where(s[1] == core, r, 0))

    return pl.pallas_call(
        functools.partial(last_kernel, scale),
        grid_spec=pltpu.PrefetchScalarGridSpec(
            num_scalar_prefetch=1,
            grid=(2,),
            in_specs=[x_spec(tokens, rows, used_by(1))] * 2
            + [x_spec(tokens, rows, used_by(0))] * 2
            + [pl.BlockSpec((2, tokens, cols), lambda r, s: (0, 0, 0))],
            out_specs=[pl.BlockSpec(shape, lambda r, s: (0, 0))] * 4,
        ),
        out_shape=[jax.ShapeDtypeStruct(shape, BF16)] * 4,
        compiler_params=params(),
        cost_estimate=QUICK,
        name="last_terms",
    )(at, *xs, v)


def seq_index(x, y, c):
    return ((x % NX) * NY + (y % NY)) * NC + c


CHIPS = [(x, y, c) for x in range(NX) for y in range(NY) for c in range(NC)]
SWAP = [(seq_index(x, y, c), seq_index(x, y, 1 - c)) for x, y, c in CHIPS]


def shift(axis, d):
    dx, dy = (d, 0) if axis == "x" else (0, d)
    return [(seq_index(x, y, c), seq_index(x + dx, y + dy, c)) for x, y, c in CHIPS]


def shift_to(axis, targets, d):
    at = {seq_index(x, y, c): (x if axis == "x" else y) for x, y, c in CHIPS}
    return [(a, b) for a, b in shift(axis, d) if at[b] in targets]


def total(parts):
    acc = parts[0].astype(F32)
    for part in parts[1:]:
        acc = acc + part.astype(F32)
    return acc.astype(BF16)


def send_all(axis, sums):
    return [lax.ppermute(sums[d], "seq", shift(axis, d)) for d in (2, 1, 3)]


def choose(pieces, targets, at):
    chosen = []
    for d in range(4):
        piece = pieces[0]
        for t, other in zip(targets[1:], pieces[1:]):
            piece = jnp.where(at == (t - d) % 4, other, piece)
        chosen.append(piece)
    return chosen


def send_to(axis, chosen, targets):
    return [lax.ppermute(chosen[d], "seq", shift_to(axis, targets, d)) for d in (2, 1, 3)]


HELD_AT_X = ((2, 1), (-2, -1), (3, 2), (-3, -2))
HELD_AT_Y = ((1, 0), (0, 0), (-1, 0), (4, None))
LAST = 3
LAST_STEP = (-3, 3)


def to_last(d):
    return [(a, b) for (x, y, c), (a, b) in zip(CHIPS, shift("y", d)) if (y + d) % NY == LAST]


def owners(turn, nz):
    pairs = []
    for x, y, c in CHIPS:
        by_x = c == turn
        r = y if by_x else x
        d = HELD_AT_X[x][0] if by_x else HELD_AT_Y[y][0]
        step = HELD_AT_X[x][1] if by_x else LAST_STEP[c] if y == LAST else 0
        for m in range(nz):
            j = (m + step) % nz
            pairs.append((seq_index(x, y, c) * nz + m, (4 * ((j - d) % nz) + r) * nz + j))
    return pairs


def per_device(layer_input, queries, keys, values, out_grad):
    tok_rows, features = queries.shape
    half = features // 2
    n_seq, n_z = lax.axis_size("seq"), lax.axis_size("head")
    scaling = 1.0 / math.sqrt(DH * tok_rows * n_seq)
    weight_scale = 1.0 / math.sqrt(tok_rows * n_seq)
    s = lax.axis_index("seq").astype(jnp.int32)
    z = lax.axis_index("head").astype(jnp.int32)
    x, y, c = s // (NY * NC), lax.rem(s // NC, NY), lax.rem(s, NC)
    core, at_x = c.reshape(1), jnp.stack([x, c])
    up = [(i, (i + 1) % n_z) for i in range(n_z)]
    down = [(i, (i - 1) % n_z) for i in range(n_z)]
    both = ("seq", "head")
    apart = [
        (seq_index(a, b, e) * n_z + m, seq_index(a, b, e) * n_z + (m + 1 - 2 * e) % n_z)
        for a, b, e in CHIPS
        for m in range(n_z)
    ]

    def go(array, way):
        return lax.ppermute(array, "head", way)

    def swap(array):
        return lax.ppermute(array, "seq", SWAP)

    def terms(xs, vs, blocks):
        return weight_terms(xs, vs, blocks, weight_scale)

    groups = {
        "x": [[seq_index(a, b, e) for a in range(NX)] for b in range(NY) for e in range(NC)],
        "y": [[seq_index(a, b, e) for b in range(NY)] for a in range(NX) for e in range(NC)],
    }

    def exchange(axis, pieces):
        return lax.all_to_all(pieces, "seq", 0, 0, axis_index_groups=groups[axis])

    prev0, next0 = go(layer_input, up), go(layer_input, down)
    kv0, g1, totals, packed = local_states(core, queries, keys, values, out_grad, n_seq)
    spread = lax.all_to_all(totals.reshape(n_seq, *totals.shape[2:]), "seq", 0, 0)
    sums = lax.all_to_all(running_sums(spread), "seq", 0, 0)
    sums = sums.reshape(*totals.shape[:2], *sums.shape[1:])
    packed = swap(packed)
    v0 = value_gradient(core, queries, keys, out_grad, packed, sums, scaling)

    u1, d1 = go(v0, up), go(v0, down)
    prev0, next0, kv0, x_own, _ = tie(prev0, next0, kv0, layer_input, v0)
    prev1, next1, own1 = swap(prev0), swap(next0), swap(x_own)
    near = [prev0, prev1, next0, next1]
    t0 = terms([x_own, own1, *near], [v0], [(0, 0), (1, 0), (2, 0)])

    p0 = exchange("x", t0)
    kv0 = tie(kv0, t0)[0]
    query_grad, key_grad = query_key_gradients(queries, keys, values, out_grad, sums, g1, kv0, scaling)

    u1, d1, query_grad, key_grad = tie(u1, d1, query_grad, key_grad)
    u2, d2 = go(u1, up), go(d1, down)
    t1 = terms(near, [d1, u1], [(0, 0), (1, 1)])
    p0 = total(list(tie(p0, t1)[0]))
    p1 = exchange("y", t1)
    c0 = choose([p0[1], p0[0], p0[2]], [0, 1, 2], y)
    y0 = send_to("y", c0, [0, 1, 2])

    u2, d2, *y0 = tie(u2, d2, *y0, t1)[:5]
    v3 = lax.ppermute(jnp.where(c == 0, u2, d2), both, apart)
    t2 = terms(near, [d2, u2], [(0, 0), (1, 1)])
    p1 = total(list(p1))
    p2 = exchange("y", t2)

    v3, p1, r0 = tie(v3, p1, total([c0[0]] + y0), t2)[:3]
    q3 = last_terms(at_x, near, v3, weight_scale)
    x3 = send_all("x", q3)
    p2 = total(list(tie(p2, q3[0])[0]))
    held = choose([p1[0], p1[1], p2[0], p2[1]], [0, 1, 2, 3], x)
    x2 = [held[0]] + send_all("x", held)
    p3 = total([q3[0]] + x3)

    p3 = tie(p3, *held)[0]
    y3 = [p3] + [lax.ppermute(p3, "seq", to_last(d)) for d in (2, 1, 3)]
    held_x = total(x2)
    first = jnp.where(c == 0, held_x, r0)
    second = jnp.where(c == 0, r0, held_x)
    r3 = total(y3)
    last = y == LAST
    first = jnp.where((c == 1) & last, r3, first)
    second = jnp.where((c == 0) & last, r3, second)
    first = lax.ppermute(first, both, owners(0, n_z))
    second = lax.ppermute(second, both, owners(1, n_z))

    away = lax.rem(z - s // 4 + n_z, n_z)
    by_x = (away == 2) | (away == 3) | (away == 5) | (away == 6)
    left = jnp.where(by_x, first, second)
    right = jnp.where(by_x, second, first)
    weight_grad = jnp.concatenate([left, right], 1).astype(F32)
    return (query_grad, key_grad, weight_grad)


def solution(mesh):
    return jax.shard_map(
        per_device,
        mesh=mesh,
        in_specs=(P("seq", "head"),) * 5,
        out_specs=(P("seq", "head"),) * 3,
        check_vma=False,
    )
```

```python
import functools
import math

import jax
import jax.numpy as jnp
from jax import lax
from jax.experimental import pallas as pl
from jax.experimental.pallas import tpu as pltpu
from jax.sharding import PartitionSpec as P

DH = 128
BLOCK = 512
HALF = BLOCK // 2
NX, NY, NC = 4, 4, 2
BF16 = jnp.bfloat16
F32 = jnp.float32

NN = (((1,), (0,)), ((), ()))
NT = (((1,), (1,)), ((), ()))
TN = (((0,), (0,)), ((), ()))


def dot(a, b, dims):
    return lax.dot_general(a, b, dims, preferred_element_type=F32)


QUICK = pl.CostEstimate(flops=1, bytes_accessed=1, transcendentals=0)


def params(mib=58):
    return pltpu.CompilerParams(vmem_limit_bytes=mib * 1024 * 1024)


def tie(*arrays):
    return lax.optimization_barrier(arrays)


def states_kernel(_, q_ref, k_ref, v_ref, o_ref, kv_ref, g_ref, tot_ref, pack_ref):
    kv = []
    g = []
    for b in range(2):
        rows = pl.ds(b * BLOCK, BLOCK)
        kv.append(dot(k_ref[rows, :], v_ref[rows, :], TN))
        g.append(dot(q_ref[rows, :], o_ref[rows, :], TN))
    kv_ref[0] = kv[0]
    g_ref[0] = g[1]
    cut = tot_ref.shape[3]
    for p in range(DH // cut):
        rows = slice(p * cut, (p + 1) * cut)
        tot_ref[0, p, 0] = (g[0] + g[1])[rows].astype(BF16)
        tot_ref[0, p, 1] = (kv[0] + kv[1])[rows].astype(BF16)

    @pl.when(pl.program_id(0) < 2)
    def _():
        for p, ref in enumerate((q_ref, k_ref, o_ref)):
            pack_ref[p] = ref[...]


def local_states(core, q, k, v, o, n_seq):
    rows, features = q.shape
    heads = features // DH
    parts = n_seq // heads

    def head(h, c):
        return lax.rem(2 * (1 - c[0]) + h, heads)

    by_head = pl.BlockSpec((rows, DH), lambda h, c: (0, head(h, c)))
    state = pl.BlockSpec((1, DH, DH), lambda h, c: (head(h, c), 0, 0))
    cuts = (parts, 2, DH // parts, DH)
    return pl.pallas_call(
        states_kernel,
        grid_spec=pltpu.PrefetchScalarGridSpec(
            num_scalar_prefetch=1,
            grid=(heads,),
            in_specs=[by_head] * 4,
            out_specs=[
                state,
                state,
                pl.BlockSpec((1, *cuts), lambda h, c: (head(h, c), 0, 0, 0, 0)),
                pl.BlockSpec((3, rows, DH), lambda h, c: (0, 0, jnp.minimum(h, 1))),
            ],
        ),
        out_shape=[
            jax.ShapeDtypeStruct((heads, DH, DH), F32),
            jax.ShapeDtypeStruct((heads, DH, DH), F32),
            jax.ShapeDtypeStruct((heads, *cuts), BF16),
            jax.ShapeDtypeStruct((3, rows, 2 * DH), BF16),
        ],
        compiler_params=params(),
        cost_estimate=QUICK,
        name="states",
    )(core, q, k, v, o)


def sums_kernel(in_ref, out_ref):
    n = in_ref.shape[0]
    for which, order in ((0, range(n - 1, -1, -1)), (1, range(n))):
        acc = jnp.zeros(in_ref.shape[2:], F32)
        for at in order:
            part = acc.astype(BF16)
            out_ref[at, which] = part
            if which == 0:
                out_ref[at ^ 1, 2] = part
            acc = acc + in_ref[at, which].astype(F32)


def running_sums(parts):
    return pl.pallas_call(
        sums_kernel,
        out_shape=jax.ShapeDtypeStruct((parts.shape[0], 3, *parts.shape[2:]), BF16),
        compiler_params=params(),
        cost_estimate=QUICK,
        name="running_sums",
    )(parts)


def keep(s0, t0, rows, cols, upper):
    s = lax.broadcasted_iota(jnp.int32, (rows, cols), 0) + s0
    t = lax.broadcasted_iota(jnp.int32, (rows, cols), 1) + t0
    return t >= s if upper else t <= s


def upper_product(a, b, c):
    top = dot(a[:HALF], b, NT)
    top = jnp.where(keep(0, 0, HALF, BLOCK, True), top, 0.0).astype(BF16)
    low = dot(a[HALF:], b[HALF:], NT)
    low = jnp.where(keep(0, 0, HALF, HALF, True), low, 0.0).astype(BF16)
    return jnp.concatenate([dot(top, c, NN), dot(low, c[HALF:], NN)], 0)


def lower_product(a, b, c):
    top = dot(a[:HALF], b[:HALF], NT)
    top = jnp.where(keep(0, 0, HALF, HALF, False), top, 0.0).astype(BF16)
    low = dot(a[HALF:], b, NT)
    low = jnp.where(keep(HALF, 0, HALF, BLOCK, False), low, 0.0).astype(BF16)
    return jnp.concatenate([dot(top, c[:HALF], NN), dot(low, c, NN)], 0)


def value_kernel(scaling, _, *refs):
    own, other = refs[:3], refs[3:6]
    own_later, other_later, out_ref = refs[6:]

    def load(members, b):
        rows = pl.ds(b * BLOCK, BLOCK)
        return [ref[rows, :] if len(ref.shape) == 2 else ref[0, rows, :] for ref in members]

    for at, (members, later) in enumerate(((own, own_later), (other, other_later))):
        after = later[0, :, 0].reshape(DH, DH).astype(F32)
        for b in (1, 0):
            q, k, o = load(members, b)
            grad = upper_product(k, q, o) + dot(k, after.astype(BF16), NN)
            out_ref[at, pl.ds(b * BLOCK, BLOCK), :] = (grad * scaling).astype(BF16)
            if b == 1:
                after = after + dot(q, o, TN)


def value_gradient(core, q, k, o, packed, sums, scaling):
    rows = q.shape[0]
    parts, cut = sums.shape[1], sums.shape[3]
    own = pl.BlockSpec((rows, DH), lambda h, c: (0, 2 * c[0] + h))
    other = [pl.BlockSpec((1, rows, DH), lambda h, c, p=p: (p, 0, h)) for p in range(3)]
    later = [
        pl.BlockSpec((1, parts, 1, cut, DH), lambda h, c, k=k: (2 * c[0] + h, 0, k, 0, 0)) for k in (0, 2)
    ]
    out = pl.BlockSpec((2, rows, DH), lambda h, c: (0, 0, h))
    return pl.pallas_call(
        functools.partial(value_kernel, scaling),
        grid_spec=pltpu.PrefetchScalarGridSpec(
            num_scalar_prefetch=1,
            grid=(2,),
            in_specs=[own] * 3 + other + later,
            out_specs=out,
        ),
        out_shape=jax.ShapeDtypeStruct((2, rows, 2 * DH), BF16),
        compiler_params=params(52),
        cost_estimate=QUICK,
        name="value_gradient",
    )(core, q, k, o, packed, packed, packed, sums, sums)


def query_key_kernel(scaling, q_ref, k_ref, v_ref, o_ref, later_ref, before_ref, g_ref, kv_ref, dq_ref, dk_ref):
    later = later_ref[0, :, 0].reshape(DH, DH).astype(F32)
    earlier = before_ref[0, :, 0].reshape(DH, DH).astype(F32)
    for b in range(2):
        rows = pl.ds(b * BLOCK, BLOCK)
        q, k, v, o = q_ref[rows, :], k_ref[rows, :], v_ref[rows, :], o_ref[rows, :]
        after = (later + g_ref[0]) if b == 0 else later
        before = earlier if b == 0 else (earlier + kv_ref[0])
        dq = lower_product(o, v, k) + dot(o, before.astype(BF16), NT)
        dk = upper_product(v, o, q) + dot(v, after.astype(BF16), NT)
        dq_ref[rows, :] = (dq * scaling).astype(BF16)
        dk_ref[rows, :] = (dk * scaling).astype(BF16)


def query_key_gradients(q, k, v, o, sums, g, kv, scaling):
    rows = q.shape[0]
    heads = q.shape[1] // DH
    parts, cut = sums.shape[1], sums.shape[3]
    by_head = pl.BlockSpec((rows, DH), lambda h: (0, h))
    state = pl.BlockSpec((1, DH, DH), lambda h: (h, 0, 0))
    later = pl.BlockSpec((1, parts, 1, cut, DH), lambda h: (h, 0, 0, 0, 0))
    earlier = pl.BlockSpec((1, parts, 1, cut, DH), lambda h: (h, 0, 1, 0, 0))
    return pl.pallas_call(
        functools.partial(query_key_kernel, scaling),
        grid=(heads,),
        in_specs=[by_head] * 4 + [later, earlier, state, state],
        out_specs=[by_head, by_head],
        out_shape=[jax.ShapeDtypeStruct(q.shape, BF16)] * 2,
        compiler_params=params(),
        cost_estimate=QUICK,
        name="query_key_gradients",
    )(q, k, v, o, sums, sums, g, kv)


def x_spec(tokens, rows, at):
    return pl.BlockSpec((tokens, rows // 2), at)


def terms_kernel(scale, blocks, n_x, n_v, *refs):
    xs, vs, out_ref = refs[:n_x], refs[n_x : n_x + n_v], refs[n_x + n_v]
    piece = out_ref.shape[2]
    for n, (x, v) in enumerate(blocks):
        term = dot(xs[2 * x][...], vs[v][0], TN) + dot(xs[2 * x + 1][...], vs[v][1], TN)
        for low in range(2):
            out_ref[low, n] = (term[low * piece : (low + 1) * piece] * scale).astype(BF16)


def weight_terms(xs, vs, blocks, scale):
    tokens, rows = xs[0].shape
    cols = vs[0].shape[2]
    tail = (len(blocks), rows // 4, cols)
    return pl.pallas_call(
        functools.partial(terms_kernel, scale, blocks, len(xs), len(vs)),
        grid=(2,),
        in_specs=[x_spec(tokens, rows, lambda r: (0, r))] * len(xs)
        + [pl.BlockSpec((2, tokens, cols), lambda r: (0, 0, 0))] * len(vs),
        out_specs=pl.BlockSpec((2, *tail), lambda r: (r, 0, 0, 0)),
        out_shape=jax.ShapeDtypeStruct((4, *tail), BF16),
        compiler_params=params(),
        cost_estimate=QUICK,
        name="weight_terms",
    )(*xs, *vs)


def last_kernel(scale, at_ref, *refs):
    xs, v_ref, outs = refs[:4], refs[4], refs[5:]
    piece = outs[0].shape[0]
    for core, pair in enumerate((xs[2:], xs[:2])):

        @pl.when(at_ref[1] == core)
        def _(pair=pair):
            term = dot(pair[0][...], v_ref[0], TN) + dot(pair[1][...], v_ref[1], TN)
            for low in range(2):
                place = lax.rem(2 * pl.program_id(0) + low + 4 - at_ref[0], 4)
                rounded = (term[low * piece : (low + 1) * piece] * scale).astype(BF16)
                for d in range(4):

                    @pl.when(place == d)
                    def _(d=d, rounded=rounded):
                        outs[d][...] = rounded


def last_terms(at, xs, v, scale):
    tokens, rows = xs[0].shape
    cols = v.shape[2]
    shape = (rows // 4, cols)

    def used_by(core):
        return lambda r, s: (0, jnp.where(s[1] == core, r, 0))

    return pl.pallas_call(
        functools.partial(last_kernel, scale),
        grid_spec=pltpu.PrefetchScalarGridSpec(
            num_scalar_prefetch=1,
            grid=(2,),
            in_specs=[x_spec(tokens, rows, used_by(1))] * 2
            + [x_spec(tokens, rows, used_by(0))] * 2
            + [pl.BlockSpec((2, tokens, cols), lambda r, s: (0, 0, 0))],
            out_specs=[pl.BlockSpec(shape, lambda r, s: (0, 0))] * 4,
        ),
        out_shape=[jax.ShapeDtypeStruct(shape, BF16)] * 4,
        compiler_params=params(52),
        cost_estimate=QUICK,
        name="last_terms",
    )(at, *xs, v)


def seq_index(x, y, c):
    return ((x % NX) * NY + (y % NY)) * NC + c


CHIPS = [(x, y, c) for x in range(NX) for y in range(NY) for c in range(NC)]
SWAP = [(seq_index(x, y, c), seq_index(x, y, 1 - c)) for x, y, c in CHIPS]


def shift(axis, d):
    dx, dy = (d, 0) if axis == "x" else (0, d)
    return [(seq_index(x, y, c), seq_index(x + dx, y + dy, c)) for x, y, c in CHIPS]


def shift_to(axis, targets, d):
    at = {seq_index(x, y, c): (x if axis == "x" else y) for x, y, c in CHIPS}
    return [(a, b) for a, b in shift(axis, d) if at[b] in targets]


def total(parts):
    acc = parts[0].astype(F32)
    for part in parts[1:]:
        acc = acc + part.astype(F32)
    return acc.astype(BF16)


def send_all(axis, sums):
    return [lax.ppermute(sums[d], "seq", shift(axis, d)) for d in (2, 1, 3)]


def choose(pieces, targets, at):
    chosen = []
    for d in range(4):
        piece = pieces[0]
        for t, other in zip(targets[1:], pieces[1:]):
            piece = jnp.where(at == (t - d) % 4, other, piece)
        chosen.append(piece)
    return chosen


def send_to(axis, chosen, targets):
    return [lax.ppermute(chosen[d], "seq", shift_to(axis, targets, d)) for d in (2, 1, 3)]


HELD_AT_X = ((2, 1), (-2, -1), (3, 2), (-3, -2))
HELD_AT_Y = ((1, 0), (0, 0), (-1, 0), (4, None))
LAST = 3
LAST_STEP = (-3, 3)


def to_last(d):
    return [(a, b) for (x, y, c), (a, b) in zip(CHIPS, shift("y", d)) if (y + d) % NY == LAST]


def owners(turn, nz):
    pairs = []
    for x, y, c in CHIPS:
        by_x = c == turn
        r = y if by_x else x
        d = HELD_AT_X[x][0] if by_x else HELD_AT_Y[y][0]
        step = HELD_AT_X[x][1] if by_x else LAST_STEP[c] if y == LAST else 0
        for m in range(nz):
            j = (m + step) % nz
            pairs.append((seq_index(x, y, c) * nz + m, (4 * ((j - d) % nz) + r) * nz + j))
    return pairs


def per_device(layer_input, queries, keys, values, out_grad):
    tok_rows, features = queries.shape
    half = features // 2
    n_seq, n_z = lax.axis_size("seq"), lax.axis_size("head")
    scaling = 1.0 / math.sqrt(DH * tok_rows * n_seq)
    weight_scale = 1.0 / math.sqrt(tok_rows * n_seq)
    s = lax.axis_index("seq").astype(jnp.int32)
    z = lax.axis_index("head").astype(jnp.int32)
    x, y, c = s // (NY * NC), lax.rem(s // NC, NY), lax.rem(s, NC)
    core, at_x = c.reshape(1), jnp.stack([x, c])
    up = [(i, (i + 1) % n_z) for i in range(n_z)]
    down = [(i, (i - 1) % n_z) for i in range(n_z)]
    both = ("seq", "head")
    apart = [
        (seq_index(a, b, e) * n_z + m, seq_index(a, b, e) * n_z + (m + 1 - 2 * e) % n_z)
        for a, b, e in CHIPS
        for m in range(n_z)
    ]

    def go(array, way):
        return lax.ppermute(array, "head", way)

    def swap(array):
        return lax.ppermute(array, "seq", SWAP)

    def terms(xs, vs, blocks):
        return weight_terms(xs, vs, blocks, weight_scale)

    groups = {
        "x": [[seq_index(a, b, e) for a in range(NX)] for b in range(NY) for e in range(NC)],
        "y": [[seq_index(a, b, e) for b in range(NY)] for a in range(NX) for e in range(NC)],
    }

    def exchange(axis, pieces):
        return lax.all_to_all(pieces, "seq", 0, 0, axis_index_groups=groups[axis])

    prev0, next0 = go(layer_input, up), go(layer_input, down)
    kv0, g1, totals, packed = local_states(core, queries, keys, values, out_grad, n_seq)
    spread = lax.all_to_all(totals.reshape(n_seq, *totals.shape[2:]), "seq", 0, 0)
    sums = lax.all_to_all(running_sums(spread), "seq", 0, 0)
    sums = sums.reshape(*totals.shape[:2], *sums.shape[1:])
    packed = swap(packed)
    v0 = value_gradient(core, queries, keys, out_grad, packed, sums, scaling)

    u1, d1 = go(v0, up), go(v0, down)
    prev0, next0, kv0, x_own, _ = tie(prev0, next0, kv0, layer_input, v0)
    prev1, next1, own1 = swap(prev0), swap(next0), swap(x_own)
    near = [prev0, prev1, next0, next1]
    t0 = terms([x_own, own1, *near], [v0], [(0, 0), (1, 0), (2, 0)])

    p0 = exchange("x", t0)
    kv0 = tie(kv0, t0)[0]
    query_grad, key_grad = query_key_gradients(queries, keys, values, out_grad, sums, g1, kv0, scaling)

    u1, d1, query_grad, key_grad = tie(u1, d1, query_grad, key_grad)
    u2, d2 = go(u1, up), go(d1, down)
    t1 = terms(near, [d1, u1], [(0, 0), (1, 1)])
    p0 = total(list(tie(p0, t1)[0]))
    p1 = exchange("y", t1)
    c0 = choose([p0[1], p0[0], p0[2]], [0, 1, 2], y)
    y0 = send_to("y", c0, [0, 1, 2])

    u2, d2, *y0 = tie(u2, d2, *y0, t1)[:5]
    v3 = lax.ppermute(jnp.where(c == 0, u2, d2), both, apart)
    t2 = terms(near, [d2, u2], [(0, 0), (1, 1)])
    p1 = total(list(p1))
    p2 = exchange("y", t2)

    v3, p1, r0 = tie(v3, p1, total([c0[0]] + y0), t2)[:3]
    q3 = last_terms(at_x, near, v3, weight_scale)
    x3 = send_all("x", q3)
    p2 = total(list(tie(p2, q3[0])[0]))
    held = choose([p1[0], p1[1], p2[0], p2[1]], [0, 1, 2, 3], x)
    x2 = [held[0]] + send_all("x", held)
    p3 = total([q3[0]] + x3)

    p3 = tie(p3, *held)[0]
    y3 = [p3] + [lax.ppermute(p3, "seq", to_last(d)) for d in (2, 1, 3)]
    held_x = total(x2)
    first = jnp.where(c == 0, held_x, r0)
    second = jnp.where(c == 0, r0, held_x)
    r3 = total(y3)
    last = y == LAST
    first = jnp.where((c == 1) & last, r3, first)
    second = jnp.where((c == 0) & last, r3, second)
    first = lax.ppermute(first, both, owners(0, n_z))
    second = lax.ppermute(second, both, owners(1, n_z))

    away = lax.rem(z - s // 4 + n_z, n_z)
    by_x = (away == 2) | (away == 3) | (away == 5) | (away == 6)
    left = jnp.where(by_x, first, second)
    right = jnp.where(by_x, second, first)
    weight_grad = jnp.concatenate([left, right], 1).astype(F32)
    return (query_grad, key_grad, weight_grad)


def solution(mesh):
    return jax.shard_map(
        per_device,
        mesh=mesh,
        in_specs=(P("seq", "head"),) * 5,
        out_specs=(P("seq", "head"),) * 3,
        check_vma=False,
    )
```
